32 devices in a mesh: rows: 16 (over z, x, core), cols: 2 (over y).
Axes of the slice: x: 2, y: 2, z: 4, core: 2. Of those that a mesh axis runs over, the one named last changes fastest.
Arguments:
- columns: float32 [16384, 1152], P('rows', 'cols'), may hold values from -4 to 4
- row_bases: float32 [4, 16384, 128], P(None, 'rows'), may hold values from -6 to 6
- order: int32 [16, 1024], P('rows'), may hold values from 0 to 1023, each once within a row
Outputs:
- solved: float32 [16384, 640], P('rows', 'cols')
The draws below stay inside these ranges and needn't reach their ends.
Inputs may be any that keep to these rules, and one draw needn't show every extreme that they name: Each row of order is a permutation of 0 to 1023.
All inputs are finite; a program needn't handle non-finite values.
Results may differ from the reference program's by a relative error of at most 0.01.
Values sent between devices are 32-bit elements; how exact they have to be, the bound alone decides.
A program may use at most 64 MiB of HBM per device.

```python
import math
import jax
import jax.numpy as jnp
from jax import lax

R = 128
LEVELS = 4
ROWS_DEV = 1024
TGT_DEV = 320
N = 16384
COLS = 1152
N_ROWS = 16
N_COLS = 2


def draw_columns(key, part):
    base = jax.random.fold_in(key, 23)
    noise_key = jax.random.fold_in(base, 0)
    noise = jax.random.normal(noise_key, (N, COLS), jnp.float32)
    return jnp.clip(noise, -4.0, 4.0)


def draw_row_bases(key, part):
    base = jax.random.fold_in(key, 11)
    noise_key, scale_key = jax.random.split(base)
    most_children = 2 ** LEVELS
    low_end, high_end = (1.35, 1.55)
    noise = jax.random.normal(noise_key, (LEVELS, N, R), jnp.float32)
    logs = jax.random.uniform(scale_key, (LEVELS, most_children), jnp.float32, math.log(low_end), math.log(high_end))
    steps = jnp.arange(LEVELS, dtype=jnp.float32)
    damping = jnp.where(steps < 0.5, 1.0, 0.3 * 0.87 ** jnp.maximum(steps - 1.0, 0.0))
    factors = jnp.exp(logs) * damping[:, None]
    points = jnp.arange(N, dtype=jnp.int32)
    row_scales = jnp.stack([factors[level][points // (N // 2 ** (LEVELS - level))] for level in range(LEVELS)])
    return jnp.clip(noise * row_scales[:, :, None], -6.0, 6.0)


def setup_inputs(seed: int = 0) -> dict:
    streams_of = jax.random.split(jax.random.key(seed), 4)
    columns = draw_columns(jax.random.fold_in(streams_of[3], 71), 0)
    row_bases = draw_row_bases(jax.random.fold_in(streams_of[3], 71), 0)
    order = jax.vmap(lambda own: jax.random.permutation(own, ROWS_DEV))(jax.random.split(streams_of[2], N_ROWS)).reshape((N_ROWS, ROWS_DEV)).astype(jnp.int32)
    return {"columns": columns, "row_bases": row_bases, "order": order}


HIGH = lax.Precision.HIGHEST

def solve_system(coupled, right_side):
    gram = jnp.einsum('...ki,...kj->...ij', coupled, coupled, precision=HIGH)
    factor = jnp.linalg.cholesky(gram)
    projected = jnp.einsum('...ki,...kq->...iq', coupled, right_side, precision=HIGH)
    middle = lax.linalg.triangular_solve(factor, projected, left_side=True, lower=True)
    return lax.linalg.triangular_solve(factor, middle, left_side=True, lower=True, transpose_a=True)

def reference(columns, row_bases, order):
    width_block = R // N_COLS
    block_cols = TGT_DEV + LEVELS * width_block
    total = ROWS_DEV * N_ROWS
    offsets = (jnp.arange(N_ROWS, dtype=jnp.int32) * ROWS_DEV)[:, None]
    places = (offsets + order.astype(jnp.int32)).reshape(-1).astype(jnp.int32)
    tree = jnp.take(columns, places, axis=0).reshape(total, N_COLS, block_cols)
    for level in range(LEVELS):
        start = TGT_DEV + (LEVELS - 1 - level) * width_block
        nodes = 2 ** (LEVELS - level - 1)
        child = total // (2 * nodes)
        scale = 0.55 / math.sqrt(R * child)
        upper = tree[:, :, :start].reshape(nodes, 2, child, N_COLS * start)
        basis = tree[:, :, start:start + width_block].reshape(nodes, 2, child, R)
        feats = row_bases[level].reshape(nodes, 2, child, R)
        proj = scale * jnp.einsum('nscr,nscq->nsrq', feats, upper, precision=HIGH)
        couple = scale * jnp.einsum('nscr,nscq->nsrq', feats, basis, precision=HIGH)
        ident = jnp.broadcast_to(jnp.eye(R, dtype=couple.dtype), (nodes, R, R))
        top = jnp.concatenate([ident, couple[:, 1]], axis=-1)
        bottom = jnp.concatenate([couple[:, 0], ident], axis=-1)
        system = jnp.concatenate([top, bottom], axis=-2)
        right_side = jnp.concatenate([proj[:, 1], proj[:, 0]], axis=-2)
        coeffs = solve_system(system, right_side).reshape(nodes, 2, R, N_COLS * start)
        update = jnp.einsum('nscr,nsrq->nscq', basis, coeffs, precision=HIGH)
        upper = (upper - update).reshape(total, N_COLS, start)
        tree = jnp.concatenate([upper, tree[:, :, start:]], axis=-1)
    targets = tree[:, :, :TGT_DEV].reshape(total, N_COLS * TGT_DEV)
    return jnp.zeros_like(targets).at[places].set(targets)
```

```python
import functools
import math

import jax
import jax.numpy as jnp
from jax import lax
from jax.experimental import pallas as pl
from jax.experimental.pallas import tpu as pltpu
from jax.sharding import PartitionSpec as P

R = 128
LEVELS = 4
TGT_DEV = 320
LANES = 128
TGT_PAD = -(-TGT_DEV // LANES) * LANES
VMEM_BYTES = 48 * 1024 * 1024
F32 = jnp.float32
BF16 = jnp.bfloat16

ROWS_ON_COLS = (((1,), (0,)), ((), ()))
COLS_ON_COLS = (((0,), (0,)), ((), ()))


def halves(value):
    high = value.astype(BF16)
    return high, (value - high.astype(F32)).astype(BF16)


def mul_halves(left, right, dims=ROWS_ON_COLS):
    def one(a, b):
        return lax.dot_general(a, b, dims, preferred_element_type=F32)

    return one(left[0], right[0]) + (one(left[0], right[1]) + one(left[1], right[0]))


def mul(left, right):
    return mul_halves(halves(left), halves(right))


def mul_full(left, right, dims=ROWS_ON_COLS):
    return lax.dot_general(
        left, right, dims, precision=lax.Precision.HIGHEST, preferred_element_type=F32
    )


def invert_two(a, b, d):
    ia = 1.0 / a
    t = b * ia
    low = 1.0 / (d - b * t)
    mid = -t * low
    return ia - t * mid, mid, low


def invert_four(d):
    e00, e01, e11 = invert_two(d[0][0], d[0][1], d[1][1])
    f00, f01, f10, f11 = d[0][2], d[0][3], d[1][2], d[1][3]
    w00, w01 = e00 * f00 + e01 * f10, e00 * f01 + e01 * f11
    w10, w11 = e01 * f00 + e11 * f10, e01 * f01 + e11 * f11
    s00 = d[2][2] - (f00 * w00 + f10 * w10)
    s01 = d[2][3] - (f00 * w01 + f10 * w11)
    s11 = d[3][3] - (f01 * w01 + f11 * w11)
    g00, g01, g11 = invert_two(s00, s01, s11)
    u00, u01 = w00 * g00 + w01 * g01, w00 * g01 + w01 * g11
    u10, u11 = w10 * g00 + w11 * g01, w10 * g01 + w11 * g11
    t00 = e00 + u00 * w00 + u01 * w01
    t01 = e01 + u00 * w10 + u01 * w11
    t11 = e11 + u10 * w10 + u11 * w11
    return [
        [t00, t01, -u00, -u01],
        [t01, t11, -u10, -u11],
        [-u00, -u10, g00, g01],
        [-u01, -u11, g01, g11],
    ]


def sweep_four(tiles, first):
    lane = lax.broadcasted_iota(jnp.int32, (8, LANES), 1)
    sub = lax.broadcasted_iota(jnp.int32, (8, LANES), 0)
    spread = [
        [jnp.broadcast_to(tile[:, first + j : first + j + 1], (8, LANES)) for j in range(4)]
        for tile in tiles
    ]
    pivot = [
        [jnp.broadcast_to(spread[0][j][first + i : first + i + 1], (8, LANES)) for j in range(4)]
        for i in range(4)
    ]
    inverse = invert_four(pivot)
    rows = [
        jnp.where(
            (lane >= first) & (lane < first + 4),
            jnp.where(lane == first + j, 1.0, 0.0),
            jnp.broadcast_to(tiles[0][first + j : first + j + 1], (8, LANES)),
        )
        for j in range(4)
    ]
    solved = [
        (inverse[i][0] * rows[0] + inverse[i][1] * rows[1])
        + (inverse[i][2] * rows[2] + inverse[i][3] * rows[3])
        for i in range(4)
    ]
    kept = (lane < first) | (lane >= first + 4)
    out = []
    for tile, cols in zip(tiles, spread):
        change = (cols[0] * solved[0] + cols[1] * solved[1]) + (
            cols[2] * solved[2] + cols[3] * solved[3]
        )
        out.append(jnp.where(kept, tile, 0.0) - change)
    for i in range(4):
        out[0] = jnp.where(sub == first + i, solved[i], out[0])
    return out


def invert_spd(gram):
    count = R // 8

    def body(_, tiles):
        tiles = sweep_four(list(tiles), 0)
        tiles = sweep_four(tiles, 4)
        tiles = tiles[1:] + tiles[:1]
        return tuple(pltpu.roll(tile, LANES - 8, 1) for tile in tiles)

    tiles = tuple(gram[8 * i : 8 * i + 8] for i in range(count))
    return jnp.concatenate(lax.fori_loop(0, count, body, tiles), axis=0)


def solve_own(own_couple, sib_couple, own_proj, sib_proj):
    row = lax.broadcasted_iota(jnp.int32, (R, R), 0)
    col = lax.broadcasted_iota(jnp.int32, (R, R), 1)
    reduced = jnp.where(row == col, 1.0, 0.0) - mul_full(sib_couple, own_couple)
    inverse = invert_spd(mul_full(reduced, reduced, COLS_ON_COLS))
    right = sib_proj - mul(sib_couple, own_proj)
    return mul_full(mul_full(inverse, reduced, (((1,), (1,)), ((), ()))), right)


def project_kernel(scales, cols_ref, basis_ref, bases_ref, order_ref, tgt_ref, own_ref):
    rows = cols_ref.shape[0]
    place = lax.broadcasted_iota(jnp.int32, (rows, rows), 0)
    pick = jnp.where(place == order_ref[...], 1.0, 0.0).astype(BF16)
    tgt = halves(cols_ref[:, :TGT_PAD])
    basis = halves(basis_ref[...])
    for level in range(LEVELS):
        high, low = halves(bases_ref[level])
        high = jnp.dot(pick, high, preferred_element_type=F32).astype(BF16)
        low = jnp.dot(pick, low, preferred_element_type=F32).astype(BF16)
        at = pl.ds(level * R, R)
        tgt_ref[at, :] = scales[level] * mul_halves((high, low), tgt, COLS_ON_COLS)
        own_ref[at, :] = scales[level] * mul_halves((high, low), basis, COLS_ON_COLS)


def project(scales, columns, basis, row_bases, order):
    return pl.pallas_call(
        functools.partial(project_kernel, scales),
        out_shape=(
            jax.ShapeDtypeStruct((LEVELS * R, TGT_PAD), F32),
            jax.ShapeDtypeStruct((LEVELS * R, basis.shape[1]), F32),
        ),
        compiler_params=pltpu.CompilerParams(vmem_limit_bytes=VMEM_BYTES),
    )(columns, basis, row_bases, order)


def spread_level(block, level, width, source):
    offset = (LEVELS - 1 - level) * width
    tile = block[:, offset // LANES * LANES : offset // LANES * LANES + LANES]
    shift = lax.rem(source * width - offset % LANES + LANES, LANES)
    lane = lax.broadcasted_iota(jnp.int32, tile.shape, 1)
    inside = (lane >= source * width) & (lane < (source + 1) * width)
    return jnp.where(inside, pltpu.roll(tile, shift, 1), 0.0)


def assemble_kernel(count, *refs):
    out_ref, width = refs[-1], R // count
    me = lax.axis_index("cols")
    for level in range(LEVELS):
        total = None
        for apart in range(count):
            part = spread_level(refs[apart][...], level, width, lax.rem(me - apart + count, count))
            total = part if total is None else total + part
        out_ref[:, level * R : (level + 1) * R] = total


def assemble(count, blocks):
    return pl.pallas_call(
        functools.partial(assemble_kernel, count),
        out_shape=jax.ShapeDtypeStruct((LEVELS * R, LEVELS * R), F32),
        compiler_params=pltpu.CompilerParams(vmem_limit_bytes=VMEM_BYTES),
    )(*blocks)


def level_kernel(own_ref, sib_ref, rest_ref, coeff_ref, out_ref):
    coeffs = solve_own(own_ref[:, :R], sib_ref[:, :R], own_ref[:, R:], sib_ref[:, R:])
    coeff_ref[...] = coeffs
    out_ref[...] = rest_ref[:, R:] - mul(rest_ref[:, :R], coeffs)


def last_kernel(own_ref, sib_ref, coeff_ref):
    coeff_ref[...] = solve_own(own_ref[:, :R], sib_ref[:, :R], own_ref[:, R:], sib_ref[:, R:])


def solve_level(own, sibling, rest):
    wide = own.shape[1] - R
    params = pltpu.CompilerParams(vmem_limit_bytes=VMEM_BYTES)
    coeff = jax.ShapeDtypeStruct((R, wide), F32)
    if rest.shape[0] == 0:
        return pl.pallas_call(last_kernel, out_shape=coeff, compiler_params=params)(own, sibling), rest
    return pl.pallas_call(
        level_kernel,
        out_shape=(coeff, jax.ShapeDtypeStruct((rest.shape[0], wide), F32)),
        compiler_params=params,
    )(own, sibling, rest)


def finish_kernel(count, *refs):
    cols_ref, coeff_refs, block_refs = refs[0], refs[1 : 1 + LEVELS], refs[1 + LEVELS : -2]
    out_ref, hold_ref = refs[-2], refs[-1]
    width = R // count
    me = lax.axis_index("cols")
    finals = [ref[:, -TGT_PAD:] for ref in coeff_refs]
    for late in range(LEVELS - 1, 0, -1):
        for early in range(late):
            at = (late - early - 1) * R
            finals[early] -= mul(coeff_refs[early][:, at : at + R], finals[late])
    for level in range(LEVELS):
        hold_ref[level] = finals[level]
    total = cols_ref[:, :TGT_PAD]
    for apart in range(count):
        source = lax.rem(me - apart + count, count)
        block = block_refs[apart][...]
        at = pl.ds(pl.multiple_of(source * width, 8), width)
        parts = [hold_ref[level, at, :] for level in range(LEVELS - 1, -1, -1)]
        if block.shape[1] > LEVELS * width:
            parts.append(jnp.zeros((block.shape[1] - LEVELS * width, TGT_PAD), F32))
        total -= mul(block, jnp.concatenate(parts, axis=0))
    out_ref[...] = total[:, :TGT_DEV]


def finish(count, columns, coeffs, blocks):
    return pl.pallas_call(
        functools.partial(finish_kernel, count),
        out_shape=jax.ShapeDtypeStruct((columns.shape[0], TGT_DEV), F32),
        scratch_shapes=[pltpu.VMEM((LEVELS, R, TGT_PAD), F32)],
        compiler_params=pltpu.CompilerParams(vmem_limit_bytes=VMEM_BYTES),
    )(columns, *coeffs, *blocks)


def partner(block, step, count):
    return lax.ppermute(block, "rows", [(i, i ^ 1 << step) for i in range(count)])


def around(block, count):
    return [block] + [
        lax.ppermute(block, "cols", [(i, (i + apart) % count) for i in range(count)])
        for apart in range(1, count)
    ]


def on_device(columns, row_bases, order):
    rows_dev = columns.shape[0]
    row_count = lax.axis_size("rows")
    col_count = lax.axis_size("cols")
    depth = row_count.bit_length() - 1
    bits = [depth - LEVELS + level for level in range(LEVELS)]
    scales = [0.55 / math.sqrt(R * rows_dev * (1 << bit)) for bit in bits]
    basis = columns[:, TGT_DEV:]
    if basis.shape[1] < LANES:
        basis = jnp.pad(basis, ((0, 0), (0, LANES - basis.shape[1])))
    tgt, own_basis = project(scales, columns, basis, row_bases, order)
    rest = jnp.concatenate([assemble(col_count, around(own_basis, col_count)), tgt], axis=1)
    blocks = around(basis, col_count)
    coeffs = []
    for level in range(LEVELS):
        own, rest = rest[:R], rest[R:]
        for step in range(bits[level]):
            own = own + partner(own, step, row_count)
        sibling = partner(own, bits[level], row_count)
        coeff, rest = solve_level(own, sibling, rest)
        coeffs.append(coeff)
    return finish(col_count, columns, coeffs, blocks)


def solution(mesh):
    placed = (P("rows", "cols"), P(None, "rows", None), P("rows", None))
    return jax.shard_map(
        on_device, mesh=mesh, in_specs=placed, out_specs=P("rows", "cols"), check_vma=False
    )
```

```python
import functools
import math

import jax
import jax.numpy as jnp
from jax import lax
from jax.experimental import pallas as pl
from jax.experimental.pallas import tpu as pltpu
from jax.sharding import PartitionSpec as P

R = 128
LEVELS = 4
TGT_DEV = 320
LANES = 128
TGT_PAD = -(-TGT_DEV // LANES) * LANES
VMEM_BYTES = 48 * 1024 * 1024
F32 = jnp.float32
BF16 = jnp.bfloat16

ROWS_ON_COLS = (((1,), (0,)), ((), ()))
COLS_ON_COLS = (((0,), (0,)), ((), ()))


def halves(value):
    high = value.astype(BF16)
    return high, (value - high.astype(F32)).astype(BF16)


def mul_halves(left, right, dims=ROWS_ON_COLS):
    def one(a, b):
        return lax.dot_general(a, b, dims, preferred_element_type=F32)

    return one(left[0], right[0]) + (one(left[0], right[1]) + one(left[1], right[0]))


def mul(left, right):
    return mul_halves(halves(left), halves(right))


def mul_full(left, right, dims=ROWS_ON_COLS):
    return lax.dot_general(
        left, right, dims, precision=lax.Precision.HIGHEST, preferred_element_type=F32
    )


def invert_two(a, b, d):
    ia = 1.0 / a
    t = b * ia
    low = 1.0 / (d - b * t)
    mid = -t * low
    return ia - t * mid, mid, low


def invert_four(d):
    e00, e01, e11 = invert_two(d[0][0], d[0][1], d[1][1])
    f00, f01, f10, f11 = d[0][2], d[0][3], d[1][2], d[1][3]
    w00, w01 = e00 * f00 + e01 * f10, e00 * f01 + e01 * f11
    w10, w11 = e01 * f00 + e11 * f10, e01 * f01 + e11 * f11
    s00 = d[2][2] - (f00 * w00 + f10 * w10)
    s01 = d[2][3] - (f00 * w01 + f10 * w11)
    s11 = d[3][3] - (f01 * w01 + f11 * w11)
    g00, g01, g11 = invert_two(s00, s01, s11)
    u00, u01 = w00 * g00 + w01 * g01, w00 * g01 + w01 * g11
    u10, u11 = w10 * g00 + w11 * g01, w10 * g01 + w11 * g11
    t00 = e00 + u00 * w00 + u01 * w01
    t01 = e01 + u00 * w10 + u01 * w11
    t11 = e11 + u10 * w10 + u11 * w11
    return [
        [t00, t01, -u00, -u01],
        [t01, t11, -u10, -u11],
        [-u00, -u10, g00, g01],
        [-u01, -u11, g01, g11],
    ]


def sweep_four(tiles, first):
    lane = lax.broadcasted_iota(jnp.int32, (8, LANES), 1)
    sub = lax.broadcasted_iota(jnp.int32, (8, LANES), 0)
    spread = [
        [jnp.broadcast_to(tile[:, first + j : first + j + 1], (8, LANES)) for j in range(4)]
        for tile in tiles
    ]
    pivot = [
        [jnp.broadcast_to(spread[0][j][first + i : first + i + 1], (8, LANES)) for j in range(4)]
        for i in range(4)
    ]
    inverse = invert_four(pivot)
    rows = [
        jnp.where(
            (lane >= first) & (lane < first + 4),
            jnp.where(lane == first + j, 1.0, 0.0),
            jnp.broadcast_to(tiles[0][first + j : first + j + 1], (8, LANES)),
        )
        for j in range(4)
    ]
    solved = [
        (inverse[i][0] * rows[0] + inverse[i][1] * rows[1])
        + (inverse[i][2] * rows[2] + inverse[i][3] * rows[3])
        for i in range(4)
    ]
    kept = (lane < first) | (lane >= first + 4)
    out = []
    for tile, cols in zip(tiles, spread):
        change = (cols[0] * solved[0] + cols[1] * solved[1]) + (
            cols[2] * solved[2] + cols[3] * solved[3]
        )
        out.append(jnp.where(kept, tile, 0.0) - change)
    for i in range(4):
        out[0] = jnp.where(sub == first + i, solved[i], out[0])
    return out


def invert_spd(gram, between):
    count = R // 8

    def body(_, tiles):
        tiles = sweep_four(list(tiles), 0)
        tiles = sweep_four(tiles, 4)
        tiles = tiles[1:] + tiles[:1]
        return tuple(pltpu.roll(tile, LANES - 8, 1) for tile in tiles)

    tiles = tuple(gram[8 * i : 8 * i + 8] for i in range(count))
    parts = len(between) + 1
    for part in range(parts):
        tiles = lax.fori_loop(count * part // parts, count * (part + 1) // parts, body, tiles)
        if part < len(between):
            between[part]()
    return jnp.concatenate(tiles, axis=0)


def project_kernel(scales, cols_ref, bases_ref, order_ref, tgt_ref, own_ref):
    rows = cols_ref.shape[1]
    place = lax.broadcasted_iota(jnp.int32, (rows, rows), 0)
    pick = jnp.where(place == order_ref[...], 1.0, 0.0).astype(BF16)
    cols = halves(cols_ref[...])
    for level in range(LEVELS):
        high, low = halves(bases_ref[level])
        high = jnp.dot(pick, high, preferred_element_type=F32).astype(BF16)
        low = jnp.dot(pick, low, preferred_element_type=F32).astype(BF16)
        at = pl.ds(level * R, R)
        found = scales[level] * mul_halves(cols, (high, low))
        tgt_ref[at, :] = found[:TGT_PAD].T
        basis = found[TGT_DEV:]
        if basis.shape[0] < LANES:
            short = LANES - basis.shape[0]
            basis = jnp.concatenate([basis, jnp.zeros((short, R), F32)], axis=0)
        own_ref[at, :] = basis.T


def project(scales, columns, row_bases, order):
    return pl.pallas_call(
        functools.partial(project_kernel, scales),
        out_shape=(
            jax.ShapeDtypeStruct((LEVELS * R, TGT_PAD), F32),
            jax.ShapeDtypeStruct((LEVELS * R, max(columns.shape[0] - TGT_DEV, LANES)), F32),
        ),
        compiler_params=pltpu.CompilerParams(vmem_limit_bytes=VMEM_BYTES),
    )(columns, row_bases, order)


def spread_level(block, level, width, source):
    offset = (LEVELS - 1 - level) * width
    tile = block[:, offset // LANES * LANES : offset // LANES * LANES + LANES]
    shift = lax.rem(source * width - offset % LANES + LANES, LANES)
    lane = lax.broadcasted_iota(jnp.int32, tile.shape, 1)
    inside = (lane >= source * width) & (lane < (source + 1) * width)
    return jnp.where(inside, pltpu.roll(tile, shift, 1), 0.0)


def sweep_kernel(row_count, col_count, bits, *refs):
    tgt_ref, own_ref, cols_ref, out_ref, blocks_ref = refs[:5]
    work, peers, mine, theirs, held, landed, own_all, sib_all = refs[5:13]
    peer_sems, block_sems, couple_sems, rest_sems, join_sems = refs[13:]
    row, col = lax.axis_index("rows"), lax.axis_index("cols")
    width, half, wide = R // col_count, R // 2, LEVELS * R + TGT_PAD
    core = lax.rem(row, 2)
    my_half = pl.ds(pl.multiple_of(core * half, half), half)
    other_half = pl.ds(pl.multiple_of((1 - core) * half, half), half)
    row_peers = []
    for step in range(row_count.bit_length() - 1):
        bit = lax.rem(row // (1 << step), 2)
        row_peers.append((row + (1 << step) * (1 - 2 * bit), col))
    col_peers = [(row, lax.rem(col + apart, col_count)) for apart in range(1, col_count)]

    def send(src, dst, sems, device):
        copy = pltpu.make_async_remote_copy(
            src_ref=src,
            dst_ref=dst,
            send_sem=sems.at[0],
            recv_sem=sems.at[1],
            device_id=device,
            device_id_type=pl.DeviceIdType.MESH,
        )
        copy.start()
        return copy

    barrier = pltpu.get_barrier_semaphore()
    for device in row_peers + col_peers:
        pl.semaphore_signal(
            barrier, inc=1, device_id=device, device_id_type=pl.DeviceIdType.MESH
        )
    pl.semaphore_wait(barrier, len(row_peers) + len(col_peers))

    def level_rows(level):
        return pl.ds(level * R, R)

    gathers = [
        [
            send(
                own_ref.at[level_rows(level)],
                peers.at[k, level_rows(level)],
                peer_sems.at[k, level],
                device,
            )
            for k, device in enumerate(col_peers)
        ]
        for level in range(LEVELS)
    ]

    def gather(level):
        at = level_rows(level)
        for copy in gathers[level]:
            copy.wait()
        blocks = [own_ref[at, :]] + [peers[k, at, :] for k in range(len(col_peers))]
        for which in range(LEVELS):
            total = None
            for apart, block in enumerate(blocks):
                source = lax.rem(col - apart + col_count, col_count)
                part = spread_level(block, which, width, source)
                total = part if total is None else total + part
            work[at, which * R : (which + 1) * R] = total

    work[:, LEVELS * R :] = tgt_ref[...]
    gather(0)
    block_copies = []
    for level in range(LEVELS):
        last = bits[level]
        at, rest = level_rows(level), wide - (level + 1) * R
        rest_cols = pl.ds((level + 1) * R, rest)

        def couple_send(step):
            return send(
                mine.at[level, step],
                theirs.at[level, step],
                couple_sems.at[level, step],
                row_peers[step],
            )

        mine[level, 0] = work[at, level * R : (level + 1) * R]
        copy = couple_send(0)
        if level > 0:
            before = pl.ds((level - 1) * R, R)
            below = pl.ds(level * R, (LEVELS - level) * R)
            work[below, rest_cols] -= mul(work[below, before], coeffs_rest)
        rest_copies = {}

        def rest_send(step, src):
            rest_copies[step] = send(
                src,
                landed.at[level, step, pl.ds(0, src.shape[0]), pl.ds(0, rest)],
                rest_sems.at[level, step],
                row_peers[step],
            )

        if last == 0:
            rest_send(0, work.at[at, rest_cols])
        else:
            rest_send(0, work.at[pl.ds(pl.multiple_of(level * R + (1 - core) * half, half), half), rest_cols])
        for step in range(last):
            copy.wait()
            mine[level, step + 1] = mine[level, step] + theirs[level, step]
            copy = couple_send(step + 1)
        copy.wait()
        own_couple, sib_couple = mine[level, last], theirs[level, last]

        def held_at(step):
            return held.at[level, step, :, pl.ds(0, rest)]

        def advance(step):
            rest_copies[step].wait()
            arrived = landed[level, step, pl.ds(0, half), pl.ds(0, rest)]
            if step == 0:
                rows = pl.ds(pl.multiple_of(level * R + core * half, half), half)
                held[level, 0, :, pl.ds(0, rest)] = work[rows, rest_cols] + arrived
            else:
                held[level, step, :, pl.ds(0, rest)] = (
                    held[level, step - 1, :, pl.ds(0, rest)] + arrived
                )
            rest_send(step + 1, held_at(step))

        joins = []

        def join():
            rest_copies[last].wait()
            ours = held_at(last - 1)
            arrived = landed.at[level, last, pl.ds(0, half), pl.ds(0, rest)]
            for k, (src, whole) in enumerate(((ours, own_all), (arrived, sib_all))):
                place = whole.at[level, my_half, pl.ds(0, rest)]
                joins.append(send(src, place, join_sems.at[level, k], row_peers[0]))
                whole[level, my_half, pl.ds(0, rest)] = src[...]

        between = [functools.partial(advance, step) for step in range(1, last)]
        if last > 0:
            advance(0)
            between.append(join)
        unit_row = lax.broadcasted_iota(jnp.int32, (R, R), 0)
        unit_col = lax.broadcasted_iota(jnp.int32, (R, R), 1)
        reduced = jnp.where(unit_row == unit_col, 1.0, 0.0) - mul_full(sib_couple, own_couple)
        inverse = invert_spd(mul_full(reduced, reduced, COLS_ON_COLS), between)
        apply = mul_full(inverse, reduced, (((1,), (1,)), ((), ())))
        if level == 0:
            for later in range(1, LEVELS):
                gather(later)
            for k, device in enumerate(col_peers):
                src = cols_ref.at[pl.ds(TGT_DEV, cols_ref.shape[0] - TGT_DEV)]
                block_copies.append(send(src, blocks_ref.at[k], block_sems.at[k], device))
        if last == 0:
            rest_copies[0].wait()
            own_proj = work[at, rest_cols]
            sib_proj = landed[level, 0, :, pl.ds(0, rest)]
        else:
            for copy in joins:
                copy.wait()
            own_proj = own_all[level, :, pl.ds(0, rest)]
            sib_proj = sib_all[level, :, pl.ds(0, rest)]

        def coeffs_of(lo, hi):
            right = sib_proj[:, lo:hi] - mul(sib_couple, own_proj[:, lo:hi])
            return mul_full(apply, right)

        if level < LEVELS - 1:
            first = coeffs_of(0, R)
            out_ref[at, :R] = first
            below = pl.ds((level + 1) * R, (LEVELS - level - 1) * R)
            work[below, (level + 1) * R : (level + 2) * R] -= mul(
                work[below, level * R : (level + 1) * R], first
            )
            coeffs_rest = coeffs_of(R, rest)
            out_ref[at, R:rest] = coeffs_rest
        else:
            out_ref[at, :rest] = coeffs_of(0, rest)
    for copy in block_copies:
        copy.wait()


def sweep(row_count, col_count, bits, tgt, own_basis, columns):
    wide, steps = LEVELS * R + TGT_PAD, row_count.bit_length() - 1
    others = max(col_count - 1, 1)
    vmem = pl.BlockSpec(memory_space=pltpu.VMEM)
    hbm = pl.BlockSpec(memory_space=pl.ANY)
    return pl.pallas_call(
        functools.partial(sweep_kernel, row_count, col_count, bits),
        out_shape=(
            jax.ShapeDtypeStruct((LEVELS * R, wide - R), F32),
            jax.ShapeDtypeStruct((others, columns.shape[0] - TGT_DEV, columns.shape[1]), F32),
        ),
        in_specs=[vmem, vmem, hbm],
        out_specs=(vmem, hbm),
        scratch_shapes=[
            pltpu.VMEM((LEVELS * R, wide), F32),
            pltpu.VMEM((others,) + own_basis.shape, F32),
            pltpu.VMEM((LEVELS, steps, R, R), F32),
            pltpu.VMEM((LEVELS, steps, R, R), F32),
            pltpu.VMEM((LEVELS, steps, R // 2, wide - R), F32),
            pltpu.VMEM((LEVELS, steps, R, wide - R), F32),
            pltpu.VMEM((LEVELS, R, wide - R), F32),
            pltpu.VMEM((LEVELS, R, wide - R), F32),
            pltpu.SemaphoreType.DMA((others, LEVELS, 2)),
            pltpu.SemaphoreType.DMA((others, 2)),
            pltpu.SemaphoreType.DMA((LEVELS, steps, 2)),
            pltpu.SemaphoreType.DMA((LEVELS, steps, 2)),
            pltpu.SemaphoreType.DMA((LEVELS, 2, 2)),
        ],
        compiler_params=pltpu.CompilerParams(
            collective_id=0, has_side_effects=True, vmem_limit_bytes=VMEM_BYTES
        ),
    )(tgt, own_basis, columns)


def finish_kernel(count, cols_ref, coeff_ref, blocks_ref, out_ref, hold_ref):
    width = R // count
    me = lax.axis_index("cols")

    def coeff(level, first, last):
        return coeff_ref[level * R : (level + 1) * R, first * R : last * R]

    tgt_tiles = TGT_PAD // R
    finals = [
        coeff(level, LEVELS - 1 - level, LEVELS - 1 - level + tgt_tiles) for level in range(LEVELS)
    ]
    for late in range(LEVELS - 1, 0, -1):
        for early in range(late):
            at = late - early - 1
            finals[early] -= mul(coeff(early, at, at + 1), finals[late])
    for level in range(LEVELS):
        hold_ref[level] = finals[level]
    total = cols_ref[:TGT_DEV]
    for apart in range(count):
        source = lax.rem(me - apart + count, count)
        block = cols_ref[TGT_DEV:] if apart == 0 else blocks_ref[apart - 1]
        at = pl.ds(pl.multiple_of(source * width, 8), width)
        parts = [hold_ref[level, at, :] for level in range(LEVELS - 1, -1, -1)]
        parts = jnp.concatenate(parts, axis=0).T[:TGT_DEV]
        total -= mul(parts, block)
    out_ref[...] = total


def finish(count, columns, coeffs, blocks):
    return pl.pallas_call(
        functools.partial(finish_kernel, count),
        out_shape=jax.ShapeDtypeStruct((TGT_DEV, columns.shape[1]), F32),
        scratch_shapes=[pltpu.VMEM((LEVELS, R, TGT_PAD), F32)],
        compiler_params=pltpu.CompilerParams(vmem_limit_bytes=VMEM_BYTES),
    )(columns, coeffs, blocks)


def on_device(columns, row_bases, order):
    rows_dev = columns.shape[0]
    row_count = lax.axis_size("rows")
    col_count = lax.axis_size("cols")
    depth = row_count.bit_length() - 1
    bits = [depth - LEVELS + level for level in range(LEVELS)]
    scales = [0.55 / math.sqrt(R * rows_dev * (1 << bit)) for bit in bits]
    columns = columns.T
    tgt, own_basis = project(scales, columns, row_bases, order)
    coeffs, blocks = sweep(row_count, col_count, bits, tgt, own_basis, columns)
    return finish(col_count, columns, coeffs, blocks).T


def solution(mesh):
    placed = (P("rows", "cols"), P(None, "rows", None), P("rows", None))
    return jax.shard_map(
        on_device, mesh=mesh, in_specs=placed, out_specs=P("rows", "cols"), check_vma=False
    )
```

```python
import functools
import math

import jax
import jax.numpy as jnp
from jax import lax
from jax.experimental import pallas as pl
from jax.experimental.pallas import tpu as pltpu
from jax.sharding import PartitionSpec as P

R = 128
LEVELS = 4
TGT_DEV = 320
LANES = 128
TGT_PAD = -(-TGT_DEV // LANES) * LANES
VMEM_BYTES = 48 * 1024 * 1024
F32 = jnp.float32
BF16 = jnp.bfloat16

ROWS_ON_COLS = (((1,), (0,)), ((), ()))
COLS_ON_COLS = (((0,), (0,)), ((), ()))


def halves(value):
    high = value.astype(BF16)
    return high, (value - high.astype(F32)).astype(BF16)


def mul_halves(left, right, dims=ROWS_ON_COLS):
    def one(a, b):
        return lax.dot_general(a, b, dims, preferred_element_type=F32)

    return one(left[0], right[0]) + (one(left[0], right[1]) + one(left[1], right[0]))


def mul(left, right):
    return mul_halves(halves(left), halves(right))


def mul_full(left, right, dims=ROWS_ON_COLS):
    return lax.dot_general(
        left, right, dims, precision=lax.Precision.HIGHEST, preferred_element_type=F32
    )


def invert_two(a, b, d):
    ia = 1.0 / a
    t = b * ia
    low = 1.0 / (d - b * t)
    mid = -t * low
    return ia - t * mid, mid, low


def invert_four(d):
    e00, e01, e11 = invert_two(d[0][0], d[0][1], d[1][1])
    f00, f01, f10, f11 = d[0][2], d[0][3], d[1][2], d[1][3]
    w00, w01 = e00 * f00 + e01 * f10, e00 * f01 + e01 * f11
    w10, w11 = e01 * f00 + e11 * f10, e01 * f01 + e11 * f11
    s00 = d[2][2] - (f00 * w00 + f10 * w10)
    s01 = d[2][3] - (f00 * w01 + f10 * w11)
    s11 = d[3][3] - (f01 * w01 + f11 * w11)
    g00, g01, g11 = invert_two(s00, s01, s11)
    u00, u01 = w00 * g00 + w01 * g01, w00 * g01 + w01 * g11
    u10, u11 = w10 * g00 + w11 * g01, w10 * g01 + w11 * g11
    t00 = e00 + u00 * w00 + u01 * w01
    t01 = e01 + u00 * w10 + u01 * w11
    t11 = e11 + u10 * w10 + u11 * w11
    return [
        [t00, t01, -u00, -u01],
        [t01, t11, -u10, -u11],
        [-u00, -u10, g00, g01],
        [-u01, -u11, g01, g11],
    ]


def sweep_four(tiles, first):
    lane = lax.broadcasted_iota(jnp.int32, (8, LANES), 1)
    sub = lax.broadcasted_iota(jnp.int32, (8, LANES), 0)
    spread = [
        [jnp.broadcast_to(tile[:, first + j : first + j + 1], (8, LANES)) for j in range(4)]
        for tile in tiles
    ]
    pivot = [
        [jnp.broadcast_to(spread[0][j][first + i : first + i + 1], (8, LANES)) for j in range(4)]
        for i in range(4)
    ]
    inverse = invert_four(pivot)
    rows = [
        jnp.where(
            (lane >= first) & (lane < first + 4),
            jnp.where(lane == first + j, 1.0, 0.0),
            jnp.broadcast_to(tiles[0][first + j : first + j + 1], (8, LANES)),
        )
        for j in range(4)
    ]
    solved = [
        (inverse[i][0] * rows[0] + inverse[i][1] * rows[1])
        + (inverse[i][2] * rows[2] + inverse[i][3] * rows[3])
        for i in range(4)
    ]
    kept = (lane < first) | (lane >= first + 4)
    out = []
    for tile, cols in zip(tiles, spread):
        change = (cols[0] * solved[0] + cols[1] * solved[1]) + (
            cols[2] * solved[2] + cols[3] * solved[3]
        )
        out.append(jnp.where(kept, tile, 0.0) - change)
    for i in range(4):
        out[0] = jnp.where(sub == first + i, solved[i], out[0])
    return out


def invert_spd(gram, between):
    count = R // 8

    def body(_, tiles):
        tiles = sweep_four(list(tiles), 0)
        tiles = sweep_four(tiles, 4)
        tiles = tiles[1:] + tiles[:1]
        return tuple(pltpu.roll(tile, LANES - 8, 1) for tile in tiles)

    tiles = tuple(gram[8 * i : 8 * i + 8] for i in range(count))
    parts = len(between) + 1
    for part in range(parts):
        tiles = lax.fori_loop(count * part // parts, count * (part + 1) // parts, body, tiles)
        if part < len(between):
            between[part]()
    return jnp.concatenate(tiles, axis=0)


def project_kernel(scales, cols_ref, bases_ref, order_ref, tgt_ref, own_ref):
    rows = cols_ref.shape[1]
    place = lax.broadcasted_iota(jnp.int32, (rows, rows), 0)
    pick = jnp.where(place == order_ref[...], 1.0, 0.0).astype(BF16)
    cols = halves(cols_ref[...])
    for level in range(LEVELS):
        high, low = halves(bases_ref[level])
        high = jnp.dot(pick, high, preferred_element_type=F32).astype(BF16)
        low = jnp.dot(pick, low, preferred_element_type=F32).astype(BF16)
        at = pl.ds(level * R, R)
        found = scales[level] * mul_halves(cols, (high, low))
        tgt_ref[at, :] = found[:TGT_PAD].T
        basis = found[TGT_DEV:]
        if basis.shape[0] < LANES:
            short = LANES - basis.shape[0]
            basis = jnp.concatenate([basis, jnp.zeros((short, R), F32)], axis=0)
        own_ref[at, :] = basis.T


def project(scales, columns, row_bases, order):
    return pl.pallas_call(
        functools.partial(project_kernel, scales),
        out_shape=(
            jax.ShapeDtypeStruct((LEVELS * R, TGT_PAD), F32),
            jax.ShapeDtypeStruct((LEVELS * R, max(columns.shape[0] - TGT_DEV, LANES)), F32),
        ),
        compiler_params=pltpu.CompilerParams(vmem_limit_bytes=VMEM_BYTES),
    )(columns, row_bases, order)


def spread_level(block, level, width, source):
    offset = (LEVELS - 1 - level) * width
    tile = block[:, offset // LANES * LANES : offset // LANES * LANES + LANES]
    shift = lax.rem(source * width - offset % LANES + LANES, LANES)
    lane = lax.broadcasted_iota(jnp.int32, tile.shape, 1)
    inside = (lane >= source * width) & (lane < (source + 1) * width)
    return jnp.where(inside, pltpu.roll(tile, shift, 1), 0.0)


def sweep_kernel(row_count, col_count, bits, *refs):
    tgt_ref, own_ref, cols_ref, out_ref, blocks_ref = refs[:5]
    state, other, early, peers = refs[5:9]
    peer_sems, block_sems, early_sems, link_sems, join_sems = refs[9:]
    row, col = lax.axis_index("rows"), lax.axis_index("cols")
    width, basis_end = R // col_count, LEVELS * R
    wide = basis_end + TGT_PAD
    core = lax.rem(row, 2)
    row_peers = []
    for step in range(row_count.bit_length() - 1):
        bit = lax.rem(row // (1 << step), 2)
        row_peers.append((row + (1 << step) * (1 - 2 * bit), col))
    col_peers = [(row, lax.rem(col + apart, col_count)) for apart in range(1, col_count)]

    def send(src, dst, sems, device):
        copy = pltpu.make_async_remote_copy(
            src_ref=src,
            dst_ref=dst,
            send_sem=sems.at[0],
            recv_sem=sems.at[1],
            device_id=device,
            device_id_type=pl.DeviceIdType.MESH,
        )
        copy.start()
        return copy

    barrier = pltpu.get_barrier_semaphore()
    for device in row_peers + col_peers:
        pl.semaphore_signal(
            barrier, inc=1, device_id=device, device_id_type=pl.DeviceIdType.MESH
        )
    pl.semaphore_wait(barrier, len(row_peers) + len(col_peers))

    def level_rows(level):
        return pl.ds(level * R, R)

    gathers = [
        [
            send(
                own_ref.at[level_rows(level)],
                peers.at[k, level_rows(level)],
                peer_sems.at[k, level],
                device,
            )
            for k, device in enumerate(col_peers)
        ]
        for level in range(LEVELS)
    ]

    def gather(level):
        at = level_rows(level)
        for copy in gathers[level]:
            copy.wait()
        blocks = [own_ref[at, :]] + [peers[k, at, :] for k in range(len(col_peers))]
        for which in range(LEVELS):
            total = None
            for apart, block in enumerate(blocks):
                source = lax.rem(col - apart + col_count, col_count)
                part = spread_level(block, which, width, source)
                total = part if total is None else total + part
            state[0, at, which * R : (which + 1) * R] = total

    def exchange(level, which, rows, cols):
        first, count = rows
        if bits[level] > 0 and which > 0:
            count = count // 2
            first = pl.multiple_of(first + core * count, R // 2)
        region = (level, pl.ds(first, count), pl.ds(*cols))
        copy = send(
            state.at[region],
            other.at[region],
            link_sems.at[level, which],
            row_peers[bits[level]],
        )
        return copy, region

    def join(level, which, sent):
        copy, region = sent
        copy.wait()
        if bits[level] == 0:
            return None
        part = other.at[region]
        return send(part, part, join_sems.at[level, which], row_peers[0])

    def joined(copy):
        if copy is not None:
            copy.wait()

    def solve(level, apply, lo, hi):
        at, mid = level_rows(level), slice(level * R, (level + 1) * R)
        own_couple, sib_couple = state[level, at, mid], other[level, at, mid]
        own_proj, sib_proj = state[level, at, lo:hi], other[level, at, lo:hi]
        own = mul(apply, sib_proj - mul(sib_couple, own_proj))
        out_ref[at, lo - (level + 1) * R : hi - (level + 1) * R] = own
        if level == LEVELS - 1:
            return
        own, sib = halves(own), halves(own_proj - mul(own_couple, own))
        for later in range(level + 1, LEVELS):
            below = level_rows(later)
            change = mul_halves(halves(state[level, below, mid]), own) + mul_halves(
                halves(other[level, below, mid]), sib
            )
            state[level + 1, below, lo:hi] = (
                state[level, below, lo:hi] + other[level, below, lo:hi] - change
            )

    state[0, :, basis_end:] = tgt_ref[...]
    gather(0)
    if bits[0] > 0:
        for level in range(1, LEVELS):
            gather(level)
        for step in range(bits[0]):
            copy = send(state.at[0], early.at[step], early_sems.at[step], row_peers[step])
            copy.wait()
            state[0] += early[step]

    block_copies = []
    couple = exchange(0, 0, (0, R), (0, R))
    apply = tgt_join = None
    for level in range(LEVELS):
        start, following, left = level * R, (level + 1) * R, (LEVELS - 1 - level) * R
        at, mid = level_rows(level), slice(start, following)
        right_sent = lower_sent = None

        def send_lower(level=level, following=following, left=left, start=start):
            return exchange(level, 2, (following, left), (start, left + R))

        if left > 0:
            right_sent = exchange(level, 1, (start, R), (following, left))
            if level > 0 or bits[0] > 0:
                lower_sent = send_lower()
        if level > 0:
            joined(tgt_join)
            solve(level - 1, apply, basis_end, wide)
        tgt_sent = exchange(level, 3, (start, left + R), (basis_end, TGT_PAD))
        couple[0].wait()
        own_couple, sib_couple = state[level, at, mid], other[level, at, mid]
        unit_row = lax.broadcasted_iota(jnp.int32, (R, R), 0)
        unit_col = lax.broadcasted_iota(jnp.int32, (R, R), 1)
        reduced = jnp.where(unit_row == unit_col, 1.0, 0.0) - mul_full(sib_couple, own_couple)
        sent, joins = [lower_sent], []

        def gather_rest():
            for later in range(1, LEVELS):
                gather(later)
            sent[0] = send_lower()
            src = cols_ref.at[pl.ds(TGT_DEV, cols_ref.shape[0] - TGT_DEV)]
            for k, device in enumerate(col_peers):
                block_copies.append(send(src, blocks_ref.at[k], block_sems.at[k], device))

        def join_basis(level=level, right_sent=right_sent):
            joins.append(join(level, 1, right_sent))
            joins.append(join(level, 2, sent[0]))

        between = []
        if level == 0 and bits[0] == 0:
            between = [gather_rest, lambda: None, lambda: None]
        elif left > 0:
            between = [lambda: None, lambda: None, join_basis]
        inverse = invert_spd(mul_full(reduced, reduced, COLS_ON_COLS), between)
        apply = mul_full(inverse, reduced, (((1,), (1,)), ((), ())))
        if level == 0 and bits[0] == 0:
            join_basis()
        for copy in joins:
            joined(copy)
        if left > 0:
            solve(level, apply, following, following + R)
            couple = exchange(level + 1, 0, (following, R), (following, R))
        tgt_join = join(level, 3, tgt_sent)
        if left > R:
            solve(level, apply, following + R, basis_end)
    joined(tgt_join)
    solve(LEVELS - 1, apply, basis_end, wide)
    if bits[0] > 0:
        src = cols_ref.at[pl.ds(TGT_DEV, cols_ref.shape[0] - TGT_DEV)]
        for k, device in enumerate(col_peers):
            block_copies.append(send(src, blocks_ref.at[k], block_sems.at[k], device))
    for copy in block_copies:
        copy.wait()


def sweep(row_count, col_count, bits, tgt, own_basis, columns):
    wide = LEVELS * R + TGT_PAD
    others, early = max(col_count - 1, 1), max(bits[0], 1)
    vmem = pl.BlockSpec(memory_space=pltpu.VMEM)
    hbm = pl.BlockSpec(memory_space=pl.ANY)
    return pl.pallas_call(
        functools.partial(sweep_kernel, row_count, col_count, bits),
        out_shape=(
            jax.ShapeDtypeStruct((LEVELS * R, wide - R), F32),
            jax.ShapeDtypeStruct((others, columns.shape[0] - TGT_DEV, columns.shape[1]), F32),
        ),
        in_specs=[vmem, vmem, hbm],
        out_specs=(vmem, hbm),
        scratch_shapes=[
            pltpu.VMEM((LEVELS, LEVELS * R, wide), F32),
            pltpu.VMEM((LEVELS, LEVELS * R, wide), F32),
            pltpu.VMEM((early, LEVELS * R if bits[0] else 8, wide), F32),
            pltpu.VMEM((others,) + own_basis.shape, F32),
            pltpu.SemaphoreType.DMA((others, LEVELS, 2)),
            pltpu.SemaphoreType.DMA((others, 2)),
            pltpu.SemaphoreType.DMA((early, 2)),
            pltpu.SemaphoreType.DMA((LEVELS, 4, 2)),
            pltpu.SemaphoreType.DMA((LEVELS, 4, 2)),
        ],
        compiler_params=pltpu.CompilerParams(
            collective_id=0, has_side_effects=True, vmem_limit_bytes=VMEM_BYTES
        ),
    )(tgt, own_basis, columns)


def finish_kernel(count, cols_ref, coeff_ref, blocks_ref, out_ref, hold_ref):
    width = R // count
    me = lax.axis_index("cols")

    def coeff(level, first, last):
        return coeff_ref[level * R : (level + 1) * R, first * R : last * R]

    tgt_tiles = TGT_PAD // R
    finals = [
        coeff(level, LEVELS - 1 - level, LEVELS - 1 - level + tgt_tiles) for level in range(LEVELS)
    ]
    for late in range(LEVELS - 1, 0, -1):
        for early in range(late):
            at = late - early - 1
            finals[early] -= mul(coeff(early, at, at + 1), finals[late])
    for level in range(LEVELS):
        hold_ref[level] = finals[level]
    total = cols_ref[:TGT_DEV]
    for apart in range(count):
        source = lax.rem(me - apart + count, count)
        block = cols_ref[TGT_DEV:] if apart == 0 else blocks_ref[apart - 1]
        at = pl.ds(pl.multiple_of(source * width, 8), width)
        parts = [hold_ref[level, at, :] for level in range(LEVELS - 1, -1, -1)]
        parts = jnp.concatenate(parts, axis=0).T[:TGT_DEV]
        total -= mul(parts, block)
    out_ref[...] = total


def finish(count, columns, coeffs, blocks):
    return pl.pallas_call(
        functools.partial(finish_kernel, count),
        out_shape=jax.ShapeDtypeStruct((TGT_DEV, columns.shape[1]), F32),
        scratch_shapes=[pltpu.VMEM((LEVELS, R, TGT_PAD), F32)],
        compiler_params=pltpu.CompilerParams(vmem_limit_bytes=VMEM_BYTES),
    )(columns, coeffs, blocks)


def on_device(columns, row_bases, order):
    rows_dev = columns.shape[0]
    row_count = lax.axis_size("rows")
    col_count = lax.axis_size("cols")
    depth = row_count.bit_length() - 1
    bits = [depth - LEVELS + level for level in range(LEVELS)]
    scales = [0.55 / math.sqrt(R * rows_dev * (1 << bit)) for bit in bits]
    columns = columns.T
    tgt, own_basis = project(scales, columns, row_bases, order)
    coeffs, blocks = sweep(row_count, col_count, bits, tgt, own_basis, columns)
    return finish(col_count, columns, coeffs, blocks).T


def solution(mesh):
    placed = (P("rows", "cols"), P(None, "rows", None), P("rows", None))
    return jax.shard_map(
        on_device, mesh=mesh, in_specs=placed, out_specs=P("rows", "cols"), check_vma=False
    )
```

```python
import functools
import math

import jax
import jax.numpy as jnp
from jax import lax
from jax.experimental import pallas as pl
from jax.experimental.pallas import tpu as pltpu
from jax.sharding import PartitionSpec as P

R = 128
LEVELS = 4
TGT_DEV = 320
LANES = 128
TGT_PAD = -(-TGT_DEV // LANES) * LANES
VMEM_BYTES = 48 * 1024 * 1024
F32 = jnp.float32
BF16 = jnp.bfloat16

ROWS_ON_COLS = (((1,), (0,)), ((), ()))
COLS_ON_COLS = (((0,), (0,)), ((), ()))


def halves(value):
    high = value.astype(BF16)
    return high, (value - high.astype(F32)).astype(BF16)


def mul_halves(left, right, dims=ROWS_ON_COLS):
    def one(a, b):
        return lax.dot_general(a, b, dims, preferred_element_type=F32)

    return one(left[0], right[0]) + (one(left[0], right[1]) + one(left[1], right[0]))


def mul(left, right):
    return mul_halves(halves(left), halves(right))


def mul_full(left, right, dims=ROWS_ON_COLS):
    return lax.dot_general(
        left, right, dims, precision=lax.Precision.HIGHEST, preferred_element_type=F32
    )


def invert_two(a, b, d):
    det = a * d - b * b
    over = pl.reciprocal(det, approx=True)
    over = over * (2.0 - det * over)
    over = over * (2.0 - det * over)
    return d * over, -b * over, a * over


def invert_four(d):
    e00, e01, e11 = invert_two(d[0][0], d[0][1], d[1][1])
    f00, f01, f10, f11 = d[0][2], d[0][3], d[1][2], d[1][3]
    w00, w01 = e00 * f00 + e01 * f10, e00 * f01 + e01 * f11
    w10, w11 = e01 * f00 + e11 * f10, e01 * f01 + e11 * f11
    s00 = d[2][2] - (f00 * w00 + f10 * w10)
    s01 = d[2][3] - (f00 * w01 + f10 * w11)
    s11 = d[3][3] - (f01 * w01 + f11 * w11)
    g00, g01, g11 = invert_two(s00, s01, s11)
    u00, u01 = w00 * g00 + w01 * g01, w00 * g01 + w01 * g11
    u10, u11 = w10 * g00 + w11 * g01, w10 * g01 + w11 * g11
    t00 = e00 + u00 * w00 + u01 * w01
    t01 = e01 + u00 * w10 + u01 * w11
    t11 = e11 + u10 * w10 + u11 * w11
    return [
        [t00, t01, -u00, -u01],
        [t01, t11, -u10, -u11],
        [-u00, -u10, g00, g01],
        [-u01, -u11, g01, g11],
    ]


def sweep_four(tiles, which, sub_first):
    lane = lax.broadcasted_iota(jnp.int32, (8, LANES), 1)
    sub = lax.broadcasted_iota(jnp.int32, (8, LANES), 0)
    first = 8 * which + sub_first
    spread = [
        [jnp.broadcast_to(tile[:, first + j : first + j + 1], (8, LANES)) for j in range(4)]
        for tile in tiles
    ]

    def row_of(value, i):
        return jnp.broadcast_to(value[sub_first + i : sub_first + i + 1], (8, LANES))

    pivot = [[row_of(spread[which][j], i) for j in range(4)] for i in range(4)]
    inverse = invert_four(pivot)
    inside = (lane >= first) & (lane < first + 4)
    rows = [
        jnp.where(inside, jnp.where(lane == first + j, 1.0, 0.0), row_of(tiles[which], j))
        for j in range(4)
    ]
    solved = [
        (inverse[i][0] * rows[0] + inverse[i][1] * rows[1])
        + (inverse[i][2] * rows[2] + inverse[i][3] * rows[3])
        for i in range(4)
    ]
    out = []
    for tile, cols in zip(tiles, spread):
        change = (cols[0] * solved[0] + cols[1] * solved[1]) + (
            cols[2] * solved[2] + cols[3] * solved[3]
        )
        out.append(jnp.where(inside, 0.0, tile) - change)
    for i in range(4):
        out[which] = jnp.where(sub == sub_first + i, solved[i], out[which])
    return out


def invert_spd(gram, cut, between):
    group = 2
    count = R // (8 * group)

    def body(_, tiles):
        tiles = list(tiles)
        for which in range(group):
            tiles = sweep_four(tiles, which, 0)
            tiles = sweep_four(tiles, which, 4)
        tiles = tiles[group:] + tiles[:group]
        return tuple(pltpu.roll(tile, LANES - 8 * group, 1) for tile in tiles)

    tiles = tuple(gram[8 * i : 8 * i + 8] for i in range(R // 8))
    if cut > 0:
        tiles = lax.fori_loop(0, cut, body, tiles)
        between()
    tiles = lax.fori_loop(cut, count, body, tiles)
    return jnp.concatenate(tiles, axis=0)


def project_kernel(scales, cols_hbm, bases_hbm, order_ref, tgt_ref, own_ref, cols_ref, bases_ref, sems):
    rows = cols_ref.shape[1]
    copies = [pltpu.make_async_copy(bases_hbm.at[0:2], bases_ref.at[0:2], sems.at[0])]
    copies.append(pltpu.make_async_copy(cols_hbm, cols_ref, sems.at[1]))
    copies.append(pltpu.make_async_copy(bases_hbm.at[2:4], bases_ref.at[2:4], sems.at[2]))
    for copy in copies:
        copy.start()
    place = lax.broadcasted_iota(jnp.int32, (rows, rows), 0)
    pick = jnp.where(place == order_ref[...], 1.0, 0.0).astype(BF16)
    copies[0].wait()
    cols = None
    for pair in range(0, LEVELS, 2):
        if pair > 0:
            copies[2].wait()
        both = jnp.concatenate([bases_ref[pair], bases_ref[pair + 1]], axis=1)
        high, low = halves(both)
        high = jnp.dot(pick, high, preferred_element_type=F32).astype(BF16)
        low = jnp.dot(pick, low, preferred_element_type=F32).astype(BF16)
        if cols is None:
            copies[1].wait()
            cols = halves(cols_ref[...])
        products = mul_halves(cols, (high, low))
        for level in range(pair, pair + 2):
            at = pl.ds(level * R, R)
            found = scales[level] * products[:, (level - pair) * R : (level - pair + 1) * R]
            tgt_ref[at, :] = found[:TGT_PAD].T
            basis = found[TGT_DEV:]
            if basis.shape[0] < LANES:
                short = LANES - basis.shape[0]
                basis = jnp.concatenate([basis, jnp.zeros((short, R), F32)], axis=0)
            own_ref[at, :] = basis.T


def project(scales, columns, row_bases, order):
    hbm = pl.BlockSpec(memory_space=pltpu.HBM)
    return pl.pallas_call(
        functools.partial(project_kernel, scales),
        out_shape=(
            jax.ShapeDtypeStruct((LEVELS * R, TGT_PAD), F32),
            jax.ShapeDtypeStruct((LEVELS * R, max(columns.shape[0] - TGT_DEV, LANES)), F32),
        ),
        in_specs=[hbm, hbm, pl.BlockSpec(memory_space=pltpu.VMEM)],
        scratch_shapes=[
            pltpu.VMEM(columns.shape, F32),
            pltpu.VMEM(row_bases.shape, F32),
            pltpu.SemaphoreType.DMA((3,)),
        ],
        compiler_params=pltpu.CompilerParams(vmem_limit_bytes=VMEM_BYTES),
    )(columns, row_bases, order)


def spread_level(block, level, width, source):
    offset = (LEVELS - 1 - level) * width
    tile = block[:, offset // LANES * LANES : offset // LANES * LANES + LANES]
    shift = lax.rem(source * width - offset % LANES + LANES, LANES)
    lane = lax.broadcasted_iota(jnp.int32, tile.shape, 1)
    inside = (lane >= source * width) & (lane < (source + 1) * width)
    return jnp.where(inside, pltpu.roll(tile, shift, 1), 0.0)


def sweep_kernel(row_count, col_count, bits, *refs):
    tgt_ref, own_ref, cols_ref, out_ref, blocks_ref = refs[:5]
    state, other, early, peers = refs[5:9]
    peer_sems, block_sems, early_sems, link_sems, join_sems = refs[9:]
    row, col = lax.axis_index("rows"), lax.axis_index("cols")
    width, basis_end = R // col_count, LEVELS * R
    wide = basis_end + TGT_PAD
    core = lax.rem(row, 2)
    row_peers = []
    for step in range(row_count.bit_length() - 1):
        bit = lax.rem(row // (1 << step), 2)
        row_peers.append((row + (1 << step) * (1 - 2 * bit), col))
    col_peers = [(row, lax.rem(col + apart, col_count)) for apart in range(1, col_count)]

    def send(src, dst, sems, device):
        copy = pltpu.make_async_remote_copy(
            src_ref=src,
            dst_ref=dst,
            send_sem=sems.at[0],
            recv_sem=sems.at[1],
            device_id=device,
            device_id_type=pl.DeviceIdType.MESH,
        )
        copy.start()
        return copy

    barrier = pltpu.get_barrier_semaphore()
    for device in row_peers + col_peers:
        pl.semaphore_signal(
            barrier, inc=1, device_id=device, device_id_type=pl.DeviceIdType.MESH
        )
    pl.semaphore_wait(barrier, len(row_peers) + len(col_peers))

    def level_rows(level):
        return pl.ds(level * R, R)

    gathers = [
        [
            send(
                own_ref.at[level_rows(level)],
                peers.at[k, level_rows(level)],
                peer_sems.at[k, level],
                device,
            )
            for k, device in enumerate(col_peers)
        ]
        for level in range(LEVELS)
    ]

    def gather(level):
        at = level_rows(level)
        for copy in gathers[level]:
            copy.wait()
        blocks = [own_ref[at, :]] + [peers[k, at, :] for k in range(len(col_peers))]
        for which in range(LEVELS):
            total = None
            for apart, block in enumerate(blocks):
                source = lax.rem(col - apart + col_count, col_count)
                part = spread_level(block, which, width, source)
                total = part if total is None else total + part
            state[0, at, which * R : (which + 1) * R] = total

    def exchange(level, which, rows, cols):
        first, count = rows
        if bits[level] > 0 and which > 0:
            count = count // 2
            first = pl.multiple_of(first + core * count, R // 2)
        region = (level, pl.ds(first, count), pl.ds(*cols))
        copy = send(
            state.at[region],
            other.at[region],
            link_sems.at[level, which],
            row_peers[bits[level]],
        )
        return copy, region

    def join(level, which, sent):
        copy, region = sent
        copy.wait()
        if bits[level] == 0:
            return None
        part = other.at[region]
        return send(part, part, join_sems.at[level, which], row_peers[0])

    def joined(copy):
        if copy is not None:
            copy.wait()

    def stacked(level):
        below = pl.ds((level + 1) * R, (LEVELS - 1 - level) * R)
        mid = slice(level * R, (level + 1) * R)
        return halves(
            jnp.concatenate([state[level, below, mid], other[level, below, mid]], axis=1)
        )

    def update(level, left_side, own, sib, lo, hi):
        out_ref[level_rows(level), lo - (level + 1) * R : hi - (level + 1) * R] = own
        if level < LEVELS - 1:
            below = pl.ds((level + 1) * R, (LEVELS - 1 - level) * R)
            both = halves(jnp.concatenate([own, sib], axis=0))
            state[level + 1, below, lo:hi] = (
                state[level, below, lo:hi]
                + other[level, below, lo:hi]
                - mul_halves(left_side, both)
            )

    def solve(level, whole, left_side, lo, hi):
        at = level_rows(level)
        right = jnp.concatenate([other[level, at, lo:hi], state[level, at, lo:hi]], axis=0)
        both = mul_halves(whole, halves(right))
        update(level, left_side, both[:R], both[R:], lo, hi)

    state[0, :, basis_end:] = tgt_ref[...]
    gather(0)
    if bits[0] > 0:
        for level in range(1, LEVELS):
            gather(level)
        for step in range(bits[0]):
            copy = send(state.at[0], early.at[step], early_sems.at[step], row_peers[step])
            copy.wait()
            state[0] += early[step]

    block_copies = []
    couple = exchange(0, 0, (0, R), (0, R))
    whole = left_side = tgt_join = None
    for level in range(LEVELS):
        start, following, left = level * R, (level + 1) * R, (LEVELS - 1 - level) * R
        at, mid = level_rows(level), slice(start, following)
        right_sent = lower_sent = None

        def send_lower(level=level, following=following, left=left, start=start):
            return exchange(level, 2, (following, left), (start, left + R))

        if left > 0:
            right_sent = exchange(level, 1, (start, R), (following, left))
            if level > 0 or bits[0] > 0:
                lower_sent = send_lower()
        if level > 0:
            joined(tgt_join)
            solve(level - 1, whole, left_side, basis_end, wide)
        tgt_sent = exchange(level, 3, (start, left + R), (basis_end, TGT_PAD))
        couple[0].wait()
        own_couple, sib_couple = state[level, at, mid], other[level, at, mid]
        unit_row = lax.broadcasted_iota(jnp.int32, (R, R), 0)
        unit_col = lax.broadcasted_iota(jnp.int32, (R, R), 1)
        reduced = jnp.where(unit_row == unit_col, 1.0, 0.0) - mul_full(sib_couple, own_couple)
        sent, joins = [lower_sent], []

        def gather_rest():
            for later in range(1, LEVELS):
                gather(later)
            sent[0] = send_lower()
            src = cols_ref.at[pl.ds(TGT_DEV, cols_ref.shape[0] - TGT_DEV)]
            for k, device in enumerate(col_peers):
                block_copies.append(send(src, blocks_ref.at[k], block_sems.at[k], device))

        def join_basis(level=level, right_sent=right_sent):
            joins.append(join(level, 1, right_sent))
            joins.append(join(level, 2, sent[0]))

        cut, between = 0, None
        if level == 0 and bits[0] == 0:
            cut, between = 2, gather_rest
        elif left > 0:
            cut, between = 6, join_basis
        top = jnp.max(jnp.abs(reduced), axis=0, keepdims=True)
        shrink = 1.0 / jnp.maximum(jnp.max(top, axis=1, keepdims=True), 1e-30)
        reduced = reduced * shrink
        inverse = invert_spd(mul_full(reduced, reduced, COLS_ON_COLS), cut, between)
        apply = shrink * mul_full(inverse, reduced, (((1,), (1,)), ((), ())))
        if level == 0 and bits[0] == 0:
            join_basis()
        for copy in joins:
            joined(copy)
        if left > 0:
            left_side = stacked(level)
            cols = pl.ds(following, R)
            own_proj = state[level, at, cols]
            own = mul(apply, other[level, at, cols] - mul(sib_couple, own_proj))
            sib = own_proj - mul(own_couple, own)
            update(level, left_side, own, sib, following, following + R)
            couple = exchange(level + 1, 0, (following, R), (following, R))
        tgt_join = join(level, 3, tgt_sent)
        turned = mul(apply, sib_couple)
        upper = jnp.concatenate([apply, -turned], axis=1)
        lower = -mul(own_couple, upper)
        lower = jnp.concatenate(
            [lower[:, :R], jnp.where(unit_row == unit_col, 1.0, 0.0) + lower[:, R:]], axis=1
        )
        whole = halves(jnp.concatenate([upper, lower], axis=0))
        if left > R:
            solve(level, whole, left_side, following + R, basis_end)
    joined(tgt_join)
    at = level_rows(LEVELS - 1)
    right = jnp.concatenate(
        [other[LEVELS - 1, at, basis_end:], state[LEVELS - 1, at, basis_end:]], axis=0
    )
    out_ref[at, :TGT_PAD] = mul(upper, right)
    if bits[0] > 0:
        src = cols_ref.at[pl.ds(TGT_DEV, cols_ref.shape[0] - TGT_DEV)]
        for k, device in enumerate(col_peers):
            block_copies.append(send(src, blocks_ref.at[k], block_sems.at[k], device))
    for copy in block_copies:
        copy.wait()


def sweep(row_count, col_count, bits, tgt, own_basis, columns):
    wide = LEVELS * R + TGT_PAD
    others, early = max(col_count - 1, 1), max(bits[0], 1)
    vmem = pl.BlockSpec(memory_space=pltpu.VMEM)
    hbm = pl.BlockSpec(memory_space=pl.ANY)
    return pl.pallas_call(
        functools.partial(sweep_kernel, row_count, col_count, bits),
        out_shape=(
            jax.ShapeDtypeStruct((LEVELS * R, wide - R), F32),
            jax.ShapeDtypeStruct((others, columns.shape[0] - TGT_DEV, columns.shape[1]), F32),
        ),
        in_specs=[vmem, vmem, hbm],
        out_specs=(vmem, hbm),
        scratch_shapes=[
            pltpu.VMEM((LEVELS, LEVELS * R, wide), F32),
            pltpu.VMEM((LEVELS, LEVELS * R, wide), F32),
            pltpu.VMEM((early, LEVELS * R if bits[0] else 8, wide), F32),
            pltpu.VMEM((others,) + own_basis.shape, F32),
            pltpu.SemaphoreType.DMA((others, LEVELS, 2)),
            pltpu.SemaphoreType.DMA((others, 2)),
            pltpu.SemaphoreType.DMA((early, 2)),
            pltpu.SemaphoreType.DMA((LEVELS, 4, 2)),
            pltpu.SemaphoreType.DMA((LEVELS, 4, 2)),
        ],
        compiler_params=pltpu.CompilerParams(
            collective_id=0, has_side_effects=True, vmem_limit_bytes=VMEM_BYTES
        ),
    )(tgt, own_basis, columns)


def finish_kernel(count, cols_ref, coeff_ref, blocks_ref, out_ref, hold_ref):
    width = R // count
    me = lax.axis_index("cols")

    def coeff(level, first, last):
        return coeff_ref[level * R : (level + 1) * R, first * R : last * R]

    tgt_tiles = TGT_PAD // R
    finals = [
        coeff(level, LEVELS - 1 - level, LEVELS - 1 - level + tgt_tiles) for level in range(LEVELS)
    ]
    for late in range(LEVELS - 1, 0, -1):
        for early in range(late):
            at = late - early - 1
            finals[early] -= mul(coeff(early, at, at + 1), finals[late])
    for level in range(LEVELS):
        hold_ref[level] = finals[level]
    total = cols_ref[:TGT_DEV]
    for apart in range(count):
        source = lax.rem(me - apart + count, count)
        block = cols_ref[TGT_DEV:] if apart == 0 else blocks_ref[apart - 1]
        at = pl.ds(pl.multiple_of(source * width, 8), width)
        parts = [hold_ref[level, at, :] for level in range(LEVELS - 1, -1, -1)]
        parts = jnp.concatenate(parts, axis=0).T[:TGT_DEV]
        total -= mul(parts, block)
    out_ref[...] = total


def finish(count, columns, coeffs, blocks):
    return pl.pallas_call(
        functools.partial(finish_kernel, count),
        out_shape=jax.ShapeDtypeStruct((TGT_DEV, columns.shape[1]), F32),
        scratch_shapes=[pltpu.VMEM((LEVELS, R, TGT_PAD), F32)],
        compiler_params=pltpu.CompilerParams(vmem_limit_bytes=VMEM_BYTES),
    )(columns, coeffs, blocks)


def on_device(columns, row_bases, order):
    rows_dev = columns.shape[0]
    row_count = lax.axis_size("rows")
    col_count = lax.axis_size("cols")
    depth = row_count.bit_length() - 1
    bits = [depth - LEVELS + level for level in range(LEVELS)]
    scales = [0.55 / math.sqrt(R * rows_dev * (1 << bit)) for bit in bits]
    columns = columns.T
    tgt, own_basis = project(scales, columns, row_bases, order)
    coeffs, blocks = sweep(row_count, col_count, bits, tgt, own_basis, columns)
    return finish(col_count, columns, coeffs, blocks).T


def solution(mesh):
    placed = (P("rows", "cols"), P(None, "rows", None), P("rows", None))
    return jax.shard_map(
        on_device, mesh=mesh, in_specs=placed, out_specs=P("rows", "cols"), check_vma=False
    )
```

```python
import functools
import math

import jax
import jax.numpy as jnp
from jax import lax
from jax.experimental import pallas as pl
from jax.experimental.pallas import tpu as pltpu
from jax.sharding import PartitionSpec as P

R = 128
LEVELS = 4
TGT_DEV = 320
LANES = 128
TGT_PAD = -(-TGT_DEV // LANES) * LANES
VMEM_BYTES = 48 * 1024 * 1024
PROJECT_BYTES = 62 * 1024 * 1024
F32 = jnp.float32
BF16 = jnp.bfloat16

ROWS_ON_COLS = (((1,), (0,)), ((), ()))
COLS_ON_COLS = (((0,), (0,)), ((), ()))


def halves(value):
    high = value.astype(BF16)
    return high, (value - high.astype(F32)).astype(BF16)


def mul_halves(left, right, dims=ROWS_ON_COLS):
    def one(a, b):
        return lax.dot_general(a, b, dims, preferred_element_type=F32)

    return one(left[0], right[0]) + (one(left[0], right[1]) + one(left[1], right[0]))


def mul(left, right):
    return mul_halves(halves(left), halves(right))


def mul_full(left, right, dims=ROWS_ON_COLS):
    return lax.dot_general(
        left, right, dims, precision=lax.Precision.HIGHEST, preferred_element_type=F32
    )


def invert_two(a, b, d):
    det = a * d - b * b
    over = pl.reciprocal(det, approx=True)
    over = over * (2.0 - det * over)
    over = over * (2.0 - det * over)
    return d * over, -b * over, a * over


def invert_four(d):
    e00, e01, e11 = invert_two(d[0][0], d[0][1], d[1][1])
    f00, f01, f10, f11 = d[0][2], d[0][3], d[1][2], d[1][3]
    w00, w01 = e00 * f00 + e01 * f10, e00 * f01 + e01 * f11
    w10, w11 = e01 * f00 + e11 * f10, e01 * f01 + e11 * f11
    s00 = d[2][2] - (f00 * w00 + f10 * w10)
    s01 = d[2][3] - (f00 * w01 + f10 * w11)
    s11 = d[3][3] - (f01 * w01 + f11 * w11)
    g00, g01, g11 = invert_two(s00, s01, s11)
    u00, u01 = w00 * g00 + w01 * g01, w00 * g01 + w01 * g11
    u10, u11 = w10 * g00 + w11 * g01, w10 * g01 + w11 * g11
    t00 = e00 + u00 * w00 + u01 * w01
    t01 = e01 + u00 * w10 + u01 * w11
    t11 = e11 + u10 * w10 + u11 * w11
    return [
        [t00, t01, -u00, -u01],
        [t01, t11, -u10, -u11],
        [-u00, -u10, g00, g01],
        [-u01, -u11, g01, g11],
    ]


def sweep_four(tiles, which, sub_first):
    lane = lax.broadcasted_iota(jnp.int32, (8, LANES), 1)
    sub = lax.broadcasted_iota(jnp.int32, (8, LANES), 0)
    first = 8 * which + sub_first
    spread = [
        [jnp.broadcast_to(tile[:, first + j : first + j + 1], (8, LANES)) for j in range(4)]
        for tile in tiles
    ]

    def row_of(value, i):
        return jnp.broadcast_to(value[sub_first + i : sub_first + i + 1], (8, LANES))

    pivot = [[row_of(spread[which][j], i) for j in range(4)] for i in range(4)]
    inverse = invert_four(pivot)
    inside = (lane >= first) & (lane < first + 4)
    rows = [
        jnp.where(inside, jnp.where(lane == first + j, 1.0, 0.0), row_of(tiles[which], j))
        for j in range(4)
    ]
    solved = [
        (inverse[i][0] * rows[0] + inverse[i][1] * rows[1])
        + (inverse[i][2] * rows[2] + inverse[i][3] * rows[3])
        for i in range(4)
    ]
    out = []
    for tile, cols in zip(tiles, spread):
        change = (cols[0] * solved[0] + cols[1] * solved[1]) + (
            cols[2] * solved[2] + cols[3] * solved[3]
        )
        out.append(jnp.where(inside, 0.0, tile) - change)
    for i in range(4):
        out[which] = jnp.where(sub == sub_first + i, solved[i], out[which])
    return out


def invert_spd(gram, between):
    group = 2
    count = R // (8 * group)

    def body(_, tiles):
        tiles = list(tiles)
        for which in range(group):
            tiles = sweep_four(tiles, which, 0)
            tiles = sweep_four(tiles, which, 4)
        tiles = tiles[group:] + tiles[:group]
        return tuple(pltpu.roll(tile, LANES - 8 * group, 1) for tile in tiles)

    tiles = tuple(gram[8 * i : 8 * i + 8] for i in range(R // 8))
    done = 0
    for cut, action in between:
        tiles = lax.fori_loop(done, cut, body, tiles)
        action()
        done = cut
    tiles = lax.fori_loop(done, count, body, tiles)
    return jnp.concatenate(tiles, axis=0)


def project_kernel(scales, cols_hbm, bases_hbm, order_ref, tgt_ref, own_ref, cols_ref, bases_ref, sems):
    rows = cols_ref.shape[1]
    copies = [pltpu.make_async_copy(bases_hbm.at[0:2], bases_ref.at[0:2], sems.at[0])]
    copies.append(pltpu.make_async_copy(cols_hbm, cols_ref, sems.at[1]))
    copies.append(pltpu.make_async_copy(bases_hbm.at[2:4], bases_ref.at[2:4], sems.at[2]))
    for copy in copies:
        copy.start()
    place = lax.broadcasted_iota(jnp.int32, (rows, rows), 0)
    pick = jnp.where(place == order_ref[...], 1.0, 0.0).astype(BF16)
    copies[0].wait()
    cols = None
    for pair in range(0, LEVELS, 2):
        if pair > 0:
            copies[2].wait()
        both = jnp.concatenate([bases_ref[pair], bases_ref[pair + 1]], axis=1)
        high, low = halves(both)
        high = jnp.dot(pick, high, preferred_element_type=F32).astype(BF16)
        low = jnp.dot(pick, low, preferred_element_type=F32).astype(BF16)
        if cols is None:
            copies[1].wait()
            cols = halves(cols_ref[...])
        products = mul_halves(cols, (high, low))
        for level in range(pair, pair + 2):
            at = pl.ds(level * R, R)
            found = scales[level] * products[:, (level - pair) * R : (level - pair + 1) * R]
            tgt_ref[at, :] = found[:TGT_PAD].T
            basis = found[TGT_DEV:]
            if basis.shape[0] < LANES:
                short = LANES - basis.shape[0]
                basis = jnp.concatenate([basis, jnp.zeros((short, R), F32)], axis=0)
            own_ref[at, :] = basis.T


def project(scales, columns, row_bases, order):
    hbm = pl.BlockSpec(memory_space=pltpu.HBM)
    return pl.pallas_call(
        functools.partial(project_kernel, scales),
        out_shape=(
            jax.ShapeDtypeStruct((LEVELS * R, TGT_PAD), F32),
            jax.ShapeDtypeStruct((LEVELS * R, max(columns.shape[0] - TGT_DEV, LANES)), F32),
        ),
        in_specs=[hbm, hbm, pl.BlockSpec(memory_space=pltpu.VMEM)],
        scratch_shapes=[
            pltpu.VMEM(columns.shape, F32),
            pltpu.VMEM(row_bases.shape, F32),
            pltpu.SemaphoreType.DMA((3,)),
        ],
        compiler_params=pltpu.CompilerParams(vmem_limit_bytes=PROJECT_BYTES),
    )(columns, row_bases, order)


def spread_level(block, level, width, source):
    offset = (LEVELS - 1 - level) * width
    tile = block[:, offset // LANES * LANES : offset // LANES * LANES + LANES]
    shift = lax.rem(source * width - offset % LANES + LANES, LANES)
    lane = lax.broadcasted_iota(jnp.int32, tile.shape, 1)
    inside = (lane >= source * width) & (lane < (source + 1) * width)
    return jnp.where(inside, pltpu.roll(tile, shift, 1), 0.0)


def sweep_kernel(row_count, col_count, bits, *refs):
    tgt_hbm, own_hbm, cols_ref, out_ref, blocks_ref = refs[:5]
    state, other, early, peers, own_ref = refs[5:10]
    load_sems, peer_sems, block_sems, early_sems, link_sems, join_sems = refs[10:]
    row, col = lax.axis_index("rows"), lax.axis_index("cols")
    width, basis_end = R // col_count, LEVELS * R
    wide = basis_end + TGT_PAD
    core = lax.rem(row, 2)
    row_peers = []
    for step in range(row_count.bit_length() - 1):
        bit = lax.rem(row // (1 << step), 2)
        row_peers.append((row + (1 << step) * (1 - 2 * bit), col))
    col_peers = [(row, lax.rem(col + apart, col_count)) for apart in range(1, col_count)]

    def send(src, dst, sems, device):
        copy = pltpu.make_async_remote_copy(
            src_ref=src,
            dst_ref=dst,
            send_sem=sems.at[0],
            recv_sem=sems.at[1],
            device_id=device,
            device_id_type=pl.DeviceIdType.MESH,
        )
        copy.start()
        return copy

    own_load = pltpu.make_async_copy(own_hbm, own_ref, load_sems.at[0])
    own_load.start()
    tgt_load = pltpu.make_async_copy(
        tgt_hbm, state.at[0, :, pl.ds(basis_end, TGT_PAD)], load_sems.at[1]
    )
    tgt_load.start()
    barrier = pltpu.get_barrier_semaphore()
    for device in row_peers + col_peers:
        pl.semaphore_signal(
            barrier, inc=1, device_id=device, device_id_type=pl.DeviceIdType.MESH
        )
    pl.semaphore_wait(barrier, len(row_peers) + len(col_peers))
    own_load.wait()

    def level_rows(level):
        return pl.ds(level * R, R)

    gathers = [
        [
            send(
                own_ref.at[level_rows(level)],
                peers.at[k, level_rows(level)],
                peer_sems.at[k, level],
                device,
            )
            for k, device in enumerate(col_peers)
        ]
        for level in range(LEVELS)
    ]

    def gather(level):
        at = level_rows(level)
        for copy in gathers[level]:
            copy.wait()
        blocks = [own_ref[at, :]] + [peers[k, at, :] for k in range(len(col_peers))]
        for which in range(LEVELS):
            total = None
            for apart, block in enumerate(blocks):
                source = lax.rem(col - apart + col_count, col_count)
                part = spread_level(block, which, width, source)
                total = part if total is None else total + part
            state[0, at, which * R : (which + 1) * R] = total

    def exchange(level, which, rows, cols):
        first, count = rows
        if bits[level] > 0 and which > 0:
            count = count // 2
            first = pl.multiple_of(first + core * count, R // 2)
        region = (level, pl.ds(first, count), pl.ds(*cols))
        copy = send(
            state.at[region],
            other.at[region],
            link_sems.at[level, which],
            row_peers[bits[level]],
        )
        return copy, region

    def join(level, which, sent):
        copy, region = sent
        copy.wait()
        if bits[level] == 0:
            return None
        part = other.at[region]
        return send(part, part, join_sems.at[level, which], row_peers[0])

    def joined(copy):
        if copy is not None:
            copy.wait()

    def stacked(level):
        below = pl.ds((level + 1) * R, (LEVELS - 1 - level) * R)
        mid = slice(level * R, (level + 1) * R)
        return halves(
            jnp.concatenate([state[level, below, mid], other[level, below, mid]], axis=1)
        )

    def update(level, left_side, own, sib, lo, hi):
        out_ref[level_rows(level), lo - (level + 1) * R : hi - (level + 1) * R] = own
        if level < LEVELS - 1:
            below = pl.ds((level + 1) * R, (LEVELS - 1 - level) * R)
            both = halves(jnp.concatenate([own, sib], axis=0))
            state[level + 1, below, lo:hi] = (
                state[level, below, lo:hi]
                + other[level, below, lo:hi]
                - mul_halves(left_side, both)
            )

    def solve(level, whole, left_side, lo, hi):
        at = level_rows(level)
        right = jnp.concatenate([other[level, at, lo:hi], state[level, at, lo:hi]], axis=0)
        both = mul_halves(whole, halves(right))
        update(level, left_side, both[:R], both[R:], lo, hi)

    gather(0)
    tgt_load.wait()
    if bits[0] > 0:
        for level in range(1, LEVELS):
            gather(level)
        for step in range(bits[0]):
            copy = send(state.at[0], early.at[step], early_sems.at[step], row_peers[step])
            copy.wait()
            state[0] += early[step]

    block_copies = []
    couple = exchange(0, 0, (0, R), (0, R))
    whole = left_side = tgt_join = None
    for level in range(LEVELS):
        start, following, left = level * R, (level + 1) * R, (LEVELS - 1 - level) * R
        at, mid = level_rows(level), slice(start, following)
        right_sent = lower_sent = None

        def send_lower(level=level, following=following, left=left, start=start):
            return exchange(level, 2, (following, left), (start, left + R))

        if left > 0:
            right_sent = exchange(level, 1, (start, R), (following, left))
            if level > 0 or bits[0] > 0:
                lower_sent = send_lower()
        late, tgt = level == 2, {}

        def targets(level=level, whole=whole, left_side=left_side, start=start, left=left, tgt=tgt):
            if level > 0:
                joined(tgt_join)
                solve(level - 1, whole, left_side, basis_end, wide)
            tgt["sent"] = exchange(level, 3, (start, left + R), (basis_end, TGT_PAD))

        if not late:
            targets()
        if level == 2:
            src = cols_ref.at[pl.ds(TGT_DEV, cols_ref.shape[0] - TGT_DEV)]
            for k, device in enumerate(col_peers):
                block_copies.append(send(src, blocks_ref.at[k], block_sems.at[k], device))
        couple[0].wait()
        own_couple, sib_couple = state[level, at, mid], other[level, at, mid]
        unit_row = lax.broadcasted_iota(jnp.int32, (R, R), 0)
        unit_col = lax.broadcasted_iota(jnp.int32, (R, R), 1)
        reduced = jnp.where(unit_row == unit_col, 1.0, 0.0) - mul_full(sib_couple, own_couple)
        sent, joins = [lower_sent], []

        def gather_rest():
            for later in range(1, LEVELS):
                gather(later)
            sent[0] = send_lower()

        def join_basis(level=level, right_sent=right_sent):
            joins.append(join(level, 1, right_sent))
            joins.append(join(level, 2, sent[0]))

        between = []
        if level == 0 and bits[0] == 0:
            between.append((2, gather_rest))
        elif left > 0:
            between.append((6, join_basis))
        if late:

            def join_targets(level=level, sent_before=tgt_sent):
                nonlocal tgt_join
                tgt_join = join(level - 1, 3, sent_before)

            between = [(2, join_targets), (4, targets)] + between
        top = jnp.max(jnp.abs(reduced), axis=0, keepdims=True)
        shrink = 1.0 / jnp.maximum(jnp.max(top, axis=1, keepdims=True), 1e-30)
        reduced = reduced * shrink
        inverse = invert_spd(mul_full(reduced, reduced, COLS_ON_COLS), between)
        apply = shrink * mul_full(inverse, reduced, (((1,), (1,)), ((), ())))
        if level == 0 and bits[0] == 0:
            join_basis()
        for copy in joins:
            joined(copy)
        if left > 0:
            left_side = stacked(level)
            cols = pl.ds(following, R)
            own_proj = state[level, at, cols]
            own = mul(apply, other[level, at, cols] - mul(sib_couple, own_proj))
            sib = own_proj - mul(own_couple, own)
            update(level, left_side, own, sib, following, following + R)
            couple = exchange(level + 1, 0, (following, R), (following, R))
        tgt_sent = tgt["sent"]
        if level != 1:
            tgt_join = join(level, 3, tgt_sent)
        turned = mul(apply, sib_couple)
        upper = jnp.concatenate([apply, -turned], axis=1)
        lower = -mul(own_couple, upper)
        lower = jnp.concatenate(
            [lower[:, :R], jnp.where(unit_row == unit_col, 1.0, 0.0) + lower[:, R:]], axis=1
        )
        whole = halves(jnp.concatenate([upper, lower], axis=0))
        if left > R:
            solve(level, whole, left_side, following + R, basis_end)
    joined(tgt_join)
    at = level_rows(LEVELS - 1)
    right = jnp.concatenate(
        [other[LEVELS - 1, at, basis_end:], state[LEVELS - 1, at, basis_end:]], axis=0
    )
    out_ref[at, :TGT_PAD] = mul(upper, right)
    for copy in block_copies:
        copy.wait()


def sweep(row_count, col_count, bits, tgt, own_basis, columns):
    wide = LEVELS * R + TGT_PAD
    others, early = max(col_count - 1, 1), max(bits[0], 1)
    vmem = pl.BlockSpec(memory_space=pltpu.VMEM)
    hbm = pl.BlockSpec(memory_space=pl.ANY)
    return pl.pallas_call(
        functools.partial(sweep_kernel, row_count, col_count, bits),
        out_shape=(
            jax.ShapeDtypeStruct((LEVELS * R, wide - R), F32),
            jax.ShapeDtypeStruct((others, columns.shape[0] - TGT_DEV, columns.shape[1]), F32),
        ),
        in_specs=[pl.BlockSpec(memory_space=pltpu.HBM)] * 2 + [hbm],
        out_specs=(vmem, hbm),
        scratch_shapes=[
            pltpu.VMEM((LEVELS, LEVELS * R, wide), F32),
            pltpu.VMEM((LEVELS, LEVELS * R, wide), F32),
            pltpu.VMEM((early, LEVELS * R if bits[0] else 8, wide), F32),
            pltpu.VMEM((others,) + own_basis.shape, F32),
            pltpu.VMEM(own_basis.shape, F32),
            pltpu.SemaphoreType.DMA((2,)),
            pltpu.SemaphoreType.DMA((others, LEVELS, 2)),
            pltpu.SemaphoreType.DMA((others, 2)),
            pltpu.SemaphoreType.DMA((early, 2)),
            pltpu.SemaphoreType.DMA((LEVELS, 4, 2)),
            pltpu.SemaphoreType.DMA((LEVELS, 4, 2)),
        ],
        compiler_params=pltpu.CompilerParams(
            collective_id=0, has_side_effects=True, vmem_limit_bytes=VMEM_BYTES
        ),
    )(tgt, own_basis, columns)


def finish_kernel(count, cols_ref, coeff_ref, blocks_ref, out_ref, hold_ref):
    width = R // count
    me = lax.axis_index("cols")

    def coeff(level, first, last):
        return coeff_ref[level * R : (level + 1) * R, first * R : last * R]

    tgt_tiles = TGT_PAD // R
    finals = [
        coeff(level, LEVELS - 1 - level, LEVELS - 1 - level + tgt_tiles) for level in range(LEVELS)
    ]
    for late in range(LEVELS - 1, 0, -1):
        for early in range(late):
            at = late - early - 1
            finals[early] -= mul(coeff(early, at, at + 1), finals[late])
    for level in range(LEVELS):
        hold_ref[level] = finals[level]
    total = cols_ref[:TGT_DEV]
    for apart in range(count):
        source = lax.rem(me - apart + count, count)
        block = cols_ref[TGT_DEV:] if apart == 0 else blocks_ref[apart - 1]
        at = pl.ds(pl.multiple_of(source * width, 8), width)
        parts = [hold_ref[level, at, :] for level in range(LEVELS - 1, -1, -1)]
        parts = jnp.concatenate(parts, axis=0).T[:TGT_DEV]
        total -= mul(parts, block)
    out_ref[...] = total


def finish(count, columns, coeffs, blocks):
    return pl.pallas_call(
        functools.partial(finish_kernel, count),
        out_shape=jax.ShapeDtypeStruct((TGT_DEV, columns.shape[1]), F32),
        scratch_shapes=[pltpu.VMEM((LEVELS, R, TGT_PAD), F32)],
        compiler_params=pltpu.CompilerParams(vmem_limit_bytes=VMEM_BYTES),
    )(columns, coeffs, blocks)


def on_device(columns, row_bases, order):
    rows_dev = columns.shape[0]
    row_count = lax.axis_size("rows")
    col_count = lax.axis_size("cols")
    depth = row_count.bit_length() - 1
    bits = [depth - LEVELS + level for level in range(LEVELS)]
    scales = [0.55 / math.sqrt(R * rows_dev * (1 << bit)) for bit in bits]
    columns = columns.T
    tgt, own_basis = project(scales, columns, row_bases, order)
    coeffs, blocks = sweep(row_count, col_count, bits, tgt, own_basis, columns)
    return finish(col_count, columns, coeffs, blocks).T


def solution(mesh):
    placed = (P("rows", "cols"), P(None, "rows", None), P("rows", None))
    return jax.shard_map(
        on_device, mesh=mesh, in_specs=placed, out_specs=P("rows", "cols"), check_vma=False
    )
```

```python
import functools
import math

import jax
import jax.numpy as jnp
from jax import lax
from jax.experimental import pallas as pl
from jax.experimental.pallas import tpu as pltpu
from jax.sharding import PartitionSpec as P

R = 128
LEVELS = 4
TGT_DEV = 320
LANES = 128
TGT_PAD = -(-TGT_DEV // LANES) * LANES
VMEM_BYTES = 48 * 1024 * 1024
F32 = jnp.float32
BF16 = jnp.bfloat16

ROWS_ON_COLS = (((1,), (0,)), ((), ()))
COLS_ON_COLS = (((0,), (0,)), ((), ()))


def halves(value):
    high = value.astype(BF16)
    return high, (value - high.astype(F32)).astype(BF16)


def mul_halves(left, right, dims=ROWS_ON_COLS):
    def one(a, b):
        return lax.dot_general(a, b, dims, preferred_element_type=F32)

    return one(left[0], right[0]) + (one(left[0], right[1]) + one(left[1], right[0]))


def mul(left, right):
    return mul_halves(halves(left), halves(right))


def mul_full(left, right, dims=ROWS_ON_COLS):
    return lax.dot_general(
        left, right, dims, precision=lax.Precision.HIGHEST, preferred_element_type=F32
    )


def invert_two(a, b, d):
    det = a * d - b * b
    over = pl.reciprocal(det, approx=True)
    over = over * (2.0 - det * over)
    over = over * (2.0 - det * over)
    return d * over, -b * over, a * over


def invert_four(d):
    e00, e01, e11 = invert_two(d[0][0], d[0][1], d[1][1])
    f00, f01, f10, f11 = d[0][2], d[0][3], d[1][2], d[1][3]
    w00, w01 = e00 * f00 + e01 * f10, e00 * f01 + e01 * f11
    w10, w11 = e01 * f00 + e11 * f10, e01 * f01 + e11 * f11
    s00 = d[2][2] - (f00 * w00 + f10 * w10)
    s01 = d[2][3] - (f00 * w01 + f10 * w11)
    s11 = d[3][3] - (f01 * w01 + f11 * w11)
    g00, g01, g11 = invert_two(s00, s01, s11)
    u00, u01 = w00 * g00 + w01 * g01, w00 * g01 + w01 * g11
    u10, u11 = w10 * g00 + w11 * g01, w10 * g01 + w11 * g11
    t00 = e00 + u00 * w00 + u01 * w01
    t01 = e01 + u00 * w10 + u01 * w11
    t11 = e11 + u10 * w10 + u11 * w11
    return [
        [t00, t01, -u00, -u01],
        [t01, t11, -u10, -u11],
        [-u00, -u10, g00, g01],
        [-u01, -u11, g01, g11],
    ]


def sweep_four(tiles, which, sub_first):
    lane = lax.broadcasted_iota(jnp.int32, (8, LANES), 1)
    sub = lax.broadcasted_iota(jnp.int32, (8, LANES), 0)
    first = 8 * which + sub_first
    spread = [
        [jnp.broadcast_to(tile[:, first + j : first + j + 1], (8, LANES)) for j in range(4)]
        for tile in tiles
    ]

    def row_of(value, i):
        return jnp.broadcast_to(value[sub_first + i : sub_first + i + 1], (8, LANES))

    pivot = [[row_of(spread[which][j], i) for j in range(4)] for i in range(4)]
    inverse = invert_four(pivot)
    inside = (lane >= first) & (lane < first + 4)
    rows = [
        jnp.where(inside, jnp.where(lane == first + j, 1.0, 0.0), row_of(tiles[which], j))
        for j in range(4)
    ]
    solved = [
        (inverse[i][0] * rows[0] + inverse[i][1] * rows[1])
        + (inverse[i][2] * rows[2] + inverse[i][3] * rows[3])
        for i in range(4)
    ]
    out = []
    for tile, cols in zip(tiles, spread):
        change = (cols[0] * solved[0] + cols[1] * solved[1]) + (
            cols[2] * solved[2] + cols[3] * solved[3]
        )
        out.append(jnp.where(inside, 0.0, tile) - change)
    for i in range(4):
        out[which] = jnp.where(sub == sub_first + i, solved[i], out[which])
    return out


def invert_spd(gram, between):
    group = 2
    count = R // (8 * group)

    def body(_, tiles):
        panel, others = list(tiles[:group]), tiles[group:]
        for which in range(group):
            panel = sweep_four(panel, which, 0)
            panel = sweep_four(panel, which, 4)
        lane = lax.broadcasted_iota(jnp.int32, (8, LANES), 1)
        left_side = jnp.concatenate(others, axis=0)[:, : 8 * group]
        change = mul_full(left_side, jnp.concatenate(panel, axis=0))
        others = [
            jnp.where(lane < 8 * group, 0.0, tile) - change[8 * i : 8 * i + 8]
            for i, tile in enumerate(others)
        ]
        tiles = others + panel
        return tuple(pltpu.roll(tile, LANES - 8 * group, 1) for tile in tiles)

    tiles = tuple(gram[8 * i : 8 * i + 8] for i in range(R // 8))
    done = 0
    for cut, action in between:
        tiles = lax.fori_loop(done, cut, body, tiles)
        action()
        done = cut
    tiles = lax.fori_loop(done, count, body, tiles)
    return jnp.concatenate(tiles, axis=0)


def project_kernel(scales, cols_hbm, bases_hbm, order_ref, tgt_ref, own_ref, cols_ref, bases_ref, sems):
    rows = cols_ref.shape[1]
    copies = [pltpu.make_async_copy(bases_hbm.at[0:2], bases_ref.at[0:2], sems.at[0])]
    copies.append(pltpu.make_async_copy(cols_hbm, cols_ref, sems.at[1]))
    copies.append(pltpu.make_async_copy(bases_hbm.at[2:4], bases_ref.at[2:4], sems.at[2]))
    for copy in copies:
        copy.start()
    place = lax.broadcasted_iota(jnp.int32, (rows, rows), 0)
    pick = jnp.where(place == order_ref[...], 1.0, 0.0).astype(BF16)
    copies[0].wait()
    cols = None
    for pair in range(0, LEVELS, 2):
        if pair > 0:
            copies[2].wait()
        both = jnp.concatenate([bases_ref[pair], bases_ref[pair + 1]], axis=1)
        high, low = halves(both)
        high = jnp.dot(pick, high, preferred_element_type=F32).astype(BF16)
        low = jnp.dot(pick, low, preferred_element_type=F32).astype(BF16)
        if cols is None:
            copies[1].wait()
            cols = halves(cols_ref[...])
        products = mul_halves(cols, (high, low))
        for level in range(pair, pair + 2):
            at = pl.ds(level * R, R)
            found = scales[level] * products[:, (level - pair) * R : (level - pair + 1) * R]
            tgt_ref[at, :] = found[:TGT_PAD].T
            basis = found[TGT_DEV:]
            if basis.shape[0] < LANES:
                short = LANES - basis.shape[0]
                basis = jnp.concatenate([basis, jnp.zeros((short, R), F32)], axis=0)
            own_ref[at, :] = basis.T


def project(scales, columns, row_bases, order):
    hbm = pl.BlockSpec(memory_space=pltpu.HBM)
    return pl.pallas_call(
        functools.partial(project_kernel, scales),
        out_shape=(
            jax.ShapeDtypeStruct((LEVELS * R, TGT_PAD), F32),
            jax.ShapeDtypeStruct((LEVELS * R, max(columns.shape[0] - TGT_DEV, LANES)), F32),
        ),
        in_specs=[hbm, hbm, pl.BlockSpec(memory_space=pltpu.VMEM)],
        scratch_shapes=[
            pltpu.VMEM(columns.shape, F32),
            pltpu.VMEM(row_bases.shape, F32),
            pltpu.SemaphoreType.DMA((3,)),
        ],
        compiler_params=pltpu.CompilerParams(vmem_limit_bytes=VMEM_BYTES),
    )(columns, row_bases, order)


def spread_level(block, level, width, source):
    offset = (LEVELS - 1 - level) * width
    tile = block[:, offset // LANES * LANES : offset // LANES * LANES + LANES]
    shift = lax.rem(source * width - offset % LANES + LANES, LANES)
    lane = lax.broadcasted_iota(jnp.int32, tile.shape, 1)
    inside = (lane >= source * width) & (lane < (source + 1) * width)
    return jnp.where(inside, pltpu.roll(tile, shift, 1), 0.0)


def sweep_kernel(row_count, col_count, bits, *refs):
    tgt_hbm, own_hbm, cols_ref, out_ref, blocks_ref = refs[:5]
    state, other, early, peers, own_ref = refs[5:10]
    load_sems, peer_sems, block_sems, early_sems, link_sems, join_sems = refs[10:]
    row, col = lax.axis_index("rows"), lax.axis_index("cols")
    width, basis_end = R // col_count, LEVELS * R
    wide = basis_end + TGT_PAD
    core = lax.rem(row, 2)
    row_peers = []
    for step in range(row_count.bit_length() - 1):
        bit = lax.rem(row // (1 << step), 2)
        row_peers.append((row + (1 << step) * (1 - 2 * bit), col))
    col_peers = [(row, lax.rem(col + apart, col_count)) for apart in range(1, col_count)]

    def send(src, dst, sems, device):
        copy = pltpu.make_async_remote_copy(
            src_ref=src,
            dst_ref=dst,
            send_sem=sems.at[0],
            recv_sem=sems.at[1],
            device_id=device,
            device_id_type=pl.DeviceIdType.MESH,
        )
        copy.start()
        return copy

    own_load = pltpu.make_async_copy(own_hbm, own_ref, load_sems.at[0])
    own_load.start()
    tgt_load = pltpu.make_async_copy(
        tgt_hbm, state.at[0, :, pl.ds(basis_end, TGT_PAD)], load_sems.at[1]
    )
    tgt_load.start()
    barrier = pltpu.get_barrier_semaphore()
    for device in row_peers + col_peers:
        pl.semaphore_signal(
            barrier, inc=1, device_id=device, device_id_type=pl.DeviceIdType.MESH
        )
    pl.semaphore_wait(barrier, len(row_peers) + len(col_peers))
    own_load.wait()

    def level_rows(level):
        return pl.ds(level * R, R)

    gathers = [
        [
            send(
                own_ref.at[level_rows(level)],
                peers.at[k, level_rows(level)],
                peer_sems.at[k, level],
                device,
            )
            for k, device in enumerate(col_peers)
        ]
        for level in range(LEVELS)
    ]

    def gather(level):
        at = level_rows(level)
        for copy in gathers[level]:
            copy.wait()
        blocks = [own_ref[at, :]] + [peers[k, at, :] for k in range(len(col_peers))]
        for which in range(LEVELS):
            total = None
            for apart, block in enumerate(blocks):
                source = lax.rem(col - apart + col_count, col_count)
                part = spread_level(block, which, width, source)
                total = part if total is None else total + part
            state[0, at, which * R : (which + 1) * R] = total

    def exchange(level, which, rows, cols):
        first, count = rows
        if bits[level] > 0 and which > 0:
            count = count // 2
            first = pl.multiple_of(first + core * count, R // 2)
        region = (level, pl.ds(first, count), pl.ds(*cols))
        copy = send(
            state.at[region],
            other.at[region],
            link_sems.at[level, which],
            row_peers[bits[level]],
        )
        return copy, region

    def join(level, which, sent):
        copy, region = sent
        copy.wait()
        if bits[level] == 0:
            return None
        part = other.at[region]
        return send(part, part, join_sems.at[level, which], row_peers[0])

    def joined(copy):
        if copy is not None:
            copy.wait()

    def stacked(level):
        below = pl.ds((level + 1) * R, (LEVELS - 1 - level) * R)
        mid = slice(level * R, (level + 1) * R)
        return halves(
            jnp.concatenate([state[level, below, mid], other[level, below, mid]], axis=1)
        )

    def update(level, left_side, own, sib, lo, hi):
        out_ref[level_rows(level), lo - (level + 1) * R : hi - (level + 1) * R] = own
        if level < LEVELS - 1:
            below = pl.ds((level + 1) * R, (LEVELS - 1 - level) * R)
            both = halves(jnp.concatenate([own, sib], axis=0))
            state[level + 1, below, lo:hi] = (
                state[level, below, lo:hi]
                + other[level, below, lo:hi]
                - mul_halves(left_side, both)
            )

    def solve(level, whole, left_side, lo, hi):
        at = level_rows(level)
        right = jnp.concatenate([other[level, at, lo:hi], state[level, at, lo:hi]], axis=0)
        both = mul_halves(whole, halves(right))
        update(level, left_side, both[:R], both[R:], lo, hi)

    gather(0)
    tgt_load.wait()
    if bits[0] > 0:
        for level in range(1, LEVELS):
            gather(level)
        for step in range(bits[0]):
            copy = send(state.at[0], early.at[step], early_sems.at[step], row_peers[step])
            copy.wait()
            state[0] += early[step]

    block_copies = []
    couple = exchange(0, 0, (0, R), (0, R))
    whole = left_side = tgt_join = None
    for level in range(LEVELS):
        start, following, left = level * R, (level + 1) * R, (LEVELS - 1 - level) * R
        at, mid = level_rows(level), slice(start, following)
        right_sent = lower_sent = None

        def send_lower(level=level, following=following, left=left, start=start):
            return exchange(level, 2, (following, left), (start, left + R))

        if left > 0:
            right_sent = exchange(level, 1, (start, R), (following, left))
            if level > 0 or bits[0] > 0:
                lower_sent = send_lower()
        late, tgt = level == 2, {}

        def targets(level=level, whole=whole, left_side=left_side, start=start, left=left, tgt=tgt):
            if level > 0:
                joined(tgt_join)
                solve(level - 1, whole, left_side, basis_end, wide)
            tgt["sent"] = exchange(level, 3, (start, left + R), (basis_end, TGT_PAD))

        if not late:
            targets()
        if level == 2:
            src = cols_ref.at[pl.ds(TGT_DEV, cols_ref.shape[0] - TGT_DEV)]
            for k, device in enumerate(col_peers):
                block_copies.append(send(src, blocks_ref.at[k], block_sems.at[k], device))
        couple[0].wait()
        own_couple, sib_couple = state[level, at, mid], other[level, at, mid]
        unit_row = lax.broadcasted_iota(jnp.int32, (R, R), 0)
        unit_col = lax.broadcasted_iota(jnp.int32, (R, R), 1)
        reduced = jnp.where(unit_row == unit_col, 1.0, 0.0) - mul_full(sib_couple, own_couple)
        sent, joins = [lower_sent], []

        def gather_rest():
            for later in range(1, LEVELS):
                gather(later)
            sent[0] = send_lower()

        def join_basis(level=level, right_sent=right_sent):
            joins.append(join(level, 1, right_sent))
            joins.append(join(level, 2, sent[0]))

        between = []
        if level == 0 and bits[0] == 0:
            between.append((2, gather_rest))
        elif left > 0:
            between.append((6, join_basis))
        if late:

            def join_targets(level=level, sent_before=tgt_sent):
                nonlocal tgt_join
                tgt_join = join(level - 1, 3, sent_before)

            between = [(2, join_targets), (4, targets)] + between
        top = jnp.max(jnp.abs(reduced), axis=0, keepdims=True)
        shrink = 1.0 / jnp.maximum(jnp.max(top, axis=1, keepdims=True), 1e-30)
        reduced = reduced * shrink
        inverse = invert_spd(mul_full(reduced, reduced, COLS_ON_COLS), between)
        apply = shrink * mul_full(inverse, reduced, (((1,), (1,)), ((), ())))
        if level == 0 and bits[0] == 0:
            join_basis()
        for copy in joins:
            joined(copy)
        if left > 0:
            left_side = stacked(level)
            cols = pl.ds(following, R)
            own_proj = state[level, at, cols]
            own = mul(apply, other[level, at, cols] - mul(sib_couple, own_proj))
            sib = own_proj - mul(own_couple, own)
            update(level, left_side, own, sib, following, following + R)
            couple = exchange(level + 1, 0, (following, R), (following, R))
        tgt_sent = tgt["sent"]
        if level != 1:
            tgt_join = join(level, 3, tgt_sent)
        turned = mul(apply, sib_couple)
        upper = jnp.concatenate([apply, -turned], axis=1)
        lower = -mul(own_couple, upper)
        lower = jnp.concatenate(
            [lower[:, :R], jnp.where(unit_row == unit_col, 1.0, 0.0) + lower[:, R:]], axis=1
        )
        whole = halves(jnp.concatenate([upper, lower], axis=0))
        if left > R:
            solve(level, whole, left_side, following + R, basis_end)
    joined(tgt_join)
    at = level_rows(LEVELS - 1)
    right = jnp.concatenate(
        [other[LEVELS - 1, at, basis_end:], state[LEVELS - 1, at, basis_end:]], axis=0
    )
    out_ref[at, :TGT_PAD] = mul(upper, right)
    for copy in block_copies:
        copy.wait()


def sweep(row_count, col_count, bits, tgt, own_basis, columns):
    wide = LEVELS * R + TGT_PAD
    others, early = max(col_count - 1, 1), max(bits[0], 1)
    vmem = pl.BlockSpec(memory_space=pltpu.VMEM)
    hbm = pl.BlockSpec(memory_space=pl.ANY)
    return pl.pallas_call(
        functools.partial(sweep_kernel, row_count, col_count, bits),
        out_shape=(
            jax.ShapeDtypeStruct((LEVELS * R, wide - R), F32),
            jax.ShapeDtypeStruct((others, columns.shape[0] - TGT_DEV, columns.shape[1]), F32),
        ),
        in_specs=[pl.BlockSpec(memory_space=pltpu.HBM)] * 2 + [hbm],
        out_specs=(vmem, hbm),
        scratch_shapes=[
            pltpu.VMEM((LEVELS, LEVELS * R, wide), F32),
            pltpu.VMEM((LEVELS, LEVELS * R, wide), F32),
            pltpu.VMEM((early, LEVELS * R if bits[0] else 8, wide), F32),
            pltpu.VMEM((others,) + own_basis.shape, F32),
            pltpu.VMEM(own_basis.shape, F32),
            pltpu.SemaphoreType.DMA((2,)),
            pltpu.SemaphoreType.DMA((others, LEVELS, 2)),
            pltpu.SemaphoreType.DMA((others, 2)),
            pltpu.SemaphoreType.DMA((early, 2)),
            pltpu.SemaphoreType.DMA((LEVELS, 4, 2)),
            pltpu.SemaphoreType.DMA((LEVELS, 4, 2)),
        ],
        compiler_params=pltpu.CompilerParams(
            collective_id=0, has_side_effects=True, vmem_limit_bytes=VMEM_BYTES
        ),
    )(tgt, own_basis, columns)


def finish_kernel(count, cols_ref, coeff_ref, blocks_ref, out_ref, hold_ref):
    width = R // count
    me = lax.axis_index("cols")

    def coeff(level, first, last):
        return coeff_ref[level * R : (level + 1) * R, first * R : last * R]

    tgt_tiles = TGT_PAD // R
    finals = [
        coeff(level, LEVELS - 1 - level, LEVELS - 1 - level + tgt_tiles) for level in range(LEVELS)
    ]
    for late in range(LEVELS - 1, 0, -1):
        for early in range(late):
            at = late - early - 1
            finals[early] -= mul(coeff(early, at, at + 1), finals[late])
    for level in range(LEVELS):
        hold_ref[level] = finals[level]
    total = cols_ref[:TGT_DEV]
    for apart in range(count):
        source = lax.rem(me - apart + count, count)
        block = cols_ref[TGT_DEV:] if apart == 0 else blocks_ref[apart - 1]
        at = pl.ds(pl.multiple_of(source * width, 8), width)
        parts = [hold_ref[level, at, :] for level in range(LEVELS - 1, -1, -1)]
        parts = jnp.concatenate(parts, axis=0).T[:TGT_DEV]
        total -= mul(parts, block)
    out_ref[...] = total


def finish(count, columns, coeffs, blocks):
    return pl.pallas_call(
        functools.partial(finish_kernel, count),
        out_shape=jax.ShapeDtypeStruct((TGT_DEV, columns.shape[1]), F32),
        scratch_shapes=[pltpu.VMEM((LEVELS, R, TGT_PAD), F32)],
        compiler_params=pltpu.CompilerParams(vmem_limit_bytes=VMEM_BYTES),
    )(columns, coeffs, blocks)


def on_device(columns, row_bases, order):
    rows_dev = columns.shape[0]
    row_count = lax.axis_size("rows")
    col_count = lax.axis_size("cols")
    depth = row_count.bit_length() - 1
    bits = [depth - LEVELS + level for level in range(LEVELS)]
    scales = [0.55 / math.sqrt(R * rows_dev * (1 << bit)) for bit in bits]
    columns = columns.T
    tgt, own_basis = project(scales, columns, row_bases, order)
    coeffs, blocks = sweep(row_count, col_count, bits, tgt, own_basis, columns)
    return finish(col_count, columns, coeffs, blocks).T


def solution(mesh):
    placed = (P("rows", "cols"), P(None, "rows", None), P("rows", None))
    return jax.shard_map(
        on_device, mesh=mesh, in_specs=placed, out_specs=P("rows", "cols"), check_vma=False
    )
```
